512 devices in a mesh: wide: 64 (over z_hi, x, y), narrow: 8 (over z_lo, core).
Axes of the slice: x: 4, y: 4, z: 16 (z_hi: 4, z_lo: 4; z = z_hi * 4 + z_lo), core: 2. Of those that a mesh axis runs over, the one named last changes fastest.
Arguments:
- initial_state: float32 [33554432], P(('wide', 'narrow')), may hold values from -6 to 6
- angles: float32 [3, 25], replicated, may hold values from -3.140625 to 3.140625
- pairings: int32 [3, 25], replicated, may hold values from 0 to 24, each once within a row
Outputs:
- final_state: float32 [33554432], P(('wide', 'narrow'))
The draws below stay inside these ranges and needn't reach their ends.
Inputs may be any that keep to these rules, and one draw needn't show every extreme that they name: Each row of pairings names every qubit once.
All inputs are finite; a program needn't handle non-finite values.
Results may differ from the reference program's by a relative error of at most 0.00025.
Values sent between devices are 32-bit elements; how exact they have to be, the bound alone decides.
No kernel may reach another device: no remote copies, remote signals or barrier semaphores. Data moves between devices by JAX's collectives and lax.ppermute only.
A program may use at most 64 MiB of HBM per device.

```python
import jax
import jax.numpy as jnp

LAYERS = 3
QUBITS = 25
STATE = 33554432


def steps_of(rng, extent, pieces, low, high):
    loudness, own = 1.0, jax.random.fold_in(rng, 6)
    for dim, parts in pieces:
        draws = jnp.exp(jax.random.uniform(jax.random.fold_in(own, dim), (parts,), jnp.float32, low / len(pieces), high / len(pieces)))
        loudness = loudness * jnp.repeat(draws, extent[dim] // parts).reshape([-1 if axis == dim else 1 for axis in range(len(extent))])
    return loudness


def gaussian(own_key, dims, deviation, most, cuts=(), held_as=jnp.bfloat16):
    array = deviation * jax.random.normal(own_key, dims, jnp.float32)
    if cuts:
        array = array * steps_of(own_key, dims, cuts, -0.22, 0.18)
    return jnp.clip(array, -most, most).astype(held_as)


def setup_inputs(seed: int = 0) -> dict:
    keys = jax.random.split(jax.random.key(seed), 4)
    initial_state = gaussian(keys[0], (STATE,), 1.0, 6.0, ((0, 512),), jnp.float32)
    angles = jnp.clip(jax.random.uniform(keys[1], (LAYERS, QUBITS), jnp.float32, -3.140625, 3.140625), -3.140625, 3.140625)
    pairings = jax.vmap(lambda own: jax.random.permutation(own, QUBITS))(jax.random.split(keys[2], LAYERS)).reshape((LAYERS, QUBITS)).astype(jnp.int32)
    return dict(initial_state=initial_state, angles=angles, pairings=pairings)


def rotate_qubit(amplitudes, angle_value, qubit):
    cosine = jnp.cos(angle_value / 2)
    sine_half = jnp.sin(angle_value / 2)
    view = amplitudes.reshape(-1, 2, 2 ** qubit)
    lower = view[:, 0, :]
    upper = view[:, 1, :]
    rotated = jnp.stack([cosine * lower - sine_half * upper, sine_half * lower + cosine * upper], axis=1)
    return rotated.reshape(-1)


def reference(initial_state, angles, pairings):
    amplitudes = initial_state.astype(jnp.float32)
    positions = jnp.arange(STATE, dtype=jnp.int32)
    for layer_number in range(LAYERS):
        for qubit in range(QUBITS):
            amplitudes = rotate_qubit(amplitudes, angles[layer_number, qubit], qubit)
        parity = jnp.zeros((STATE,), jnp.int32)
        for pair_number in range(QUBITS // 2):
            first_qubit = pairings[layer_number, 2 * pair_number].astype(jnp.int32)
            second_qubit = pairings[layer_number, 2 * pair_number + 1].astype(jnp.int32)
            joint_bits = jnp.right_shift(positions, first_qubit) & jnp.right_shift(positions, second_qubit) & 1
            parity = parity + joint_bits
        amplitudes = jnp.where(parity % 2 == 1, -amplitudes, amplitudes)
    return amplitudes
```

```python
import jax
import jax.numpy as jnp
from jax import lax
from jax.experimental import pallas as pl
from jax.experimental.pallas import tpu as pltpu
from jax.sharding import PartitionSpec as P

SIDE = 256
LANES = 128
CORE = 16
PAIRS = 12
AXES = ("wide", "narrow")


def trig(angle):
    t = angle * 0.5
    u = t * t
    sine = 1.0 / 6227020800
    for term in (-1.0 / 39916800, 1.0 / 362880, -1.0 / 5040, 1.0 / 120, -1.0 / 6, 1.0):
        sine = sine * u + term
    cosine = -1.0 / 87178291200
    for term in (1.0 / 479001600, -1.0 / 3628800, 1.0 / 40320, -1.0 / 720, 1.0 / 24, -0.5, 1.0):
        cosine = cosine * u + term
    return cosine, sine * t


def iota(shape, axis):
    return lax.broadcasted_iota(jnp.int32, shape, axis)


def choose(pairings):
    bad = jnp.int32(0)
    hot = jnp.int32(0)
    one = jnp.int32(1)
    for k in range(PAIRS):
        p, r = pairings[1, 2 * k], pairings[1, 2 * k + 1]
        p_bit, r_bit = lax.shift_left(one, p), lax.shift_left(one, r)
        bad = bad | jnp.where(p > CORE, r_bit, 0) | jnp.where(r > CORE, p_bit, 0)
        hot = hot | jnp.where(p == CORE, r_bit, 0) | jnp.where(r == CORE, p_bit, 0)
    free = ~bad & 255
    trades = []
    for position in range(8, 16):
        calm = free & ~hot
        pool = jnp.where(calm != 0, calm, free)
        taken = jnp.where(((bad >> position) & 1) == 1, pool & -pool, 0)
        free = free & ~taken
        trades.append(taken)
    for position in range(8, 16):
        calm = free & ~hot
        taken = jnp.where(((hot >> position) & 1) == 1, calm & -calm, 0)
        free = free & ~taken
        trades[position - 8] = trades[position - 8] | taken
    left = jnp.int32(0)
    for position in range(8, 16):
        taken = trades[position - 8]
        stays = jnp.where(taken == 0, lax.shift_left(one, jnp.int32(position)), taken)
        left = left | (stays & hot)
    return trades, jnp.where(left != 0, 1, 0)


def qubits_at(trades):
    table = []
    for column in range(8):
        held = jnp.int32(column)
        for position in range(8, 16):
            held = jnp.where(trades[position - 8] == 1 << column, position, held)
        table.append(held)
    for position in range(8, 16):
        taken = trades[position - 8]
        held = jnp.int32(0)
        for column in range(1, 8):
            held = held + jnp.where(taken >= 1 << column, 1, 0)
        table.append(jnp.where(taken == 0, position, held))
    return table


def angle_table(entries):
    place = iota((8, LANES), 0) * LANES + iota((8, LANES), 1)
    table = jnp.zeros((8, LANES), jnp.float32)
    for row, lane, value in entries:
        table = jnp.where(place == row * LANES + lane, value, table)
    return table


def bit_masks():
    i, j = iota((LANES, LANES), 0), iota((LANES, LANES), 1)
    same = [((i ^ j) >> b) & 1 == 0 for b in range(7)]
    upper = [(i >> b) & 1 == 1 for b in range(7)]
    return same, upper


def kron_matrix(masks, cosines, sines, row, base, transposed):
    same, upper = masks
    total = None
    for b in range(7):
        c = cosines[row : row + 1, base + b : base + b + 1]
        s = sines[row : row + 1, base + b : base + b + 1]
        if transposed:
            s = -s
        factor = jnp.where(same[b], c, jnp.where(upper[b], s, -s))
        total = factor if total is None else total * factor
    c = cosines[row : row + 1, base + 7 : base + 8]
    s = sines[row : row + 1, base + 7 : base + 8]
    if transposed:
        s = -s
    top = jnp.concatenate([total * c, total * -s], axis=1)
    low = jnp.concatenate([total * s, total * c], axis=1)
    return jnp.concatenate([top, low], axis=0)


def parts(value):
    high = value.astype(jnp.bfloat16)
    low = (value - high.astype(jnp.float32)).astype(jnp.bfloat16)
    return high, low


def product(left, right):
    (lh, ll), (rh, rl) = left, right

    def dot(a, b):
        return jnp.dot(a, b, preferred_element_type=jnp.float32)

    return dot(lh, rh) + (dot(lh, rl) + dot(ll, rh))


def load_matrix(ref):
    return jnp.concatenate(
        [ref[pl.ds(0, SIDE, stride=2), :], ref[pl.ds(1, SIDE, stride=2), :]], axis=1
    )


def store_matrix(ref, value):
    ref[pl.ds(0, SIDE, stride=2), :] = value[:, :LANES]
    ref[pl.ds(1, SIDE, stride=2), :] = value[:, LANES:]


def trade_bits(work, trades):
    lane = iota((SIDE, LANES), 1)
    row = iota((SIDE, LANES), 0)
    for bit in range(8):
        taken = trades[bit]
        step = 1 << bit
        row_up = (row & step) != 0

        @pl.when((taken != 0) & (taken < LANES))
        def _():
            lane_up = (lane & taken) != 0
            for half in range(2):
                columns = slice(half * LANES, half * LANES + LANES)
                held = work[:, columns]
                later = pltpu.roll(held, SIDE - step, 0)
                sooner = pltpu.roll(held, step, 0)
                from_later = pltpu.roll(later, taken, 1)
                from_sooner = pltpu.roll(sooner, LANES - taken, 1)
                moved = jnp.where(lane_up, from_later, from_sooner)
                work[:, columns] = jnp.where(row_up == lane_up, held, moved)

        @pl.when(taken == LANES)
        def _():
            first = work[:, :LANES]
            second = work[:, LANES:]
            work[:, :LANES] = jnp.where(row_up, pltpu.roll(second, step, 0), first)
            work[:, LANES:] = jnp.where(row_up, second, pltpu.roll(first, SIDE - step, 0))


def first_kernel(angles, pairings, state, out, work):
    table = angle_table([(0, q, angles[0, q]) for q in range(16)])
    cosines, sines = trig(table)
    masks = bit_masks()
    rows = parts(kron_matrix(masks, cosines, sines, 0, 8, False))
    columns = parts(kron_matrix(masks, cosines, sines, 0, 0, True))
    value = load_matrix(state)
    value = product(rows, parts(value))
    work[...] = product(parts(value), columns)
    trades, _ = choose(pairings)
    trade_bits(work, trades)
    store_matrix(out, work[...])


def signs(index, pairings, layer, place, keep=None):
    parity = jnp.zeros(index.shape, jnp.int32)
    for k in range(PAIRS):
        p, r = place(pairings[layer, 2 * k]), place(pairings[layer, 2 * k + 1])
        if keep is not None:
            p = jnp.where(keep(p, r), p, 31)
        parity = parity ^ (lax.shift_right_logical(index, p) & lax.shift_right_logical(index, r))
    return 1.0 - 2.0 * (parity & 1).astype(jnp.float32)


CHIP_1, CHIP_2, COLUMN_2, CHIP_3, ROW_2, ROW_3, COLUMN_3 = range(7)
MINE_1, OTHER_1, MINE_2, OTHER_2, MINE_LATE, OTHER_LATE, LAST = range(7)


def prepare_kernel(angles, pairings, high, low, sign, coefficients, flag, places):
    trades, needed = choose(pairings)
    flag[0] = needed
    held = qubits_at(trades)
    for position in range(16):
        places[position] = held[position]
    for position in range(16, 25):
        places[position] = jnp.int32(position)
    entries = []
    for layer in range(3):
        entries += [(layer, p, angles[layer, held[p]]) for p in range(16)]
        entries += [(layer, p, angles[layer, p]) for p in range(16, 25)]
    cosines, sines = trig(angle_table(entries))
    masks = bit_masks()
    for slot, layer, base, transposed in (
        (CHIP_1, 0, 17, False),
        (CHIP_2, 1, 17, False),
        (COLUMN_2, 1, 0, True),
        (CHIP_3, 2, 17, False),
        (ROW_2, 1, 8, False),
        (ROW_3, 2, 8, False),
        (COLUMN_3, 2, 0, True),
    ):
        high[slot], low[slot] = parts(
            kron_matrix(masks, cosines, sines, layer, base, transposed)
        )
    wide, narrow = lax.axis_index("wide"), lax.axis_index("narrow")
    chip = wide * 4 + lax.shift_right_logical(narrow, 1)
    core = narrow & 1
    turn = jnp.where(core == 1, sines, -sines)
    coefficients[0:8, :] = cosines
    coefficients[8:16, :] = turn
    local = iota((SIDE, SIDE), 0) * SIDE + iota((SIDE, SIDE), 1) + lax.shift_left(chip, 17)
    mine = local + lax.shift_left(core, 16)
    other = local + lax.shift_left(1 - core, 16)

    def outer(q):
        return places[q]

    def inner(q):
        place = places[q]
        moved = jnp.where(place > CORE, place - 9, place + 9)
        return jnp.where((place < 8) | (place == CORE), place, moved)

    def in_rows(place):
        return (place >= 8) & (place < 16)

    def late(p, r):
        return in_rows(p) | in_rows(r)

    def early(p, r):
        return (p <= CORE) & (r <= CORE)

    sign[MINE_1] = signs(mine, pairings, 0, inner)
    sign[OTHER_1] = signs(other, pairings, 0, inner)
    sign[MINE_2] = signs(mine, pairings, 1, inner, early)
    sign[OTHER_2] = signs(other, pairings, 1, inner, early)
    sign[MINE_LATE] = signs(mine, pairings, 1, outer, late)
    sign[OTHER_LATE] = signs(other, pairings, 1, outer, late)
    sign[LAST] = signs(mine, pairings, 2, outer)


def core_turn(coefficients, layer):
    c = coefficients[layer : layer + 1, CORE : CORE + 1]
    s = coefficients[8 + layer : 9 + layer, CORE : CORE + 1]
    return c, s


def second_kernel(flag, mine_ref, other_ref, high, low, sign, coefficients, out, spare):
    def matrix(slot):
        return high[slot], low[slot]

    mine = product(matrix(CHIP_1), parts(load_matrix(mine_ref)))
    other = product(matrix(CHIP_1), parts(load_matrix(other_ref)))
    c, s = core_turn(coefficients, 0)
    mine, other = c * mine + s * other, c * other - s * mine
    mine, other = mine * sign[MINE_1], other * sign[OTHER_1]
    c, s = core_turn(coefficients, 1)
    mine, other = c * mine + s * other, c * other - s * mine
    mine = product(matrix(CHIP_2), parts(mine))
    other = product(matrix(CHIP_2), parts(other))
    mine = product(parts(mine), matrix(COLUMN_2)) * sign[MINE_2]
    other = product(parts(other), matrix(COLUMN_2)) * sign[OTHER_2]
    c, s = core_turn(coefficients, 2)
    waits = jnp.full((1, 1), flag[0], jnp.int32) == 1
    c, s = jnp.where(waits, 1.0, c), jnp.where(waits, 0.0, s)
    mine = c * mine + s * other
    store_matrix(out, product(matrix(CHIP_3), parts(mine)))


def third_kernel(pairings, flag, mine_ref, other_ref, high, low, sign, coefficients, out, work):
    def matrix(slot):
        return high[slot], low[slot]

    trades, _ = choose(pairings)
    mine = product(matrix(ROW_2), parts(load_matrix(mine_ref)))
    work[...] = mine * sign[MINE_LATE]

    @pl.when(flag[0] == 1)
    def _():
        other = product(matrix(ROW_2), parts(load_matrix(other_ref))) * sign[OTHER_LATE]
        c, s = core_turn(coefficients, 2)
        work[...] = c * work[...] + s * other

    mine = product(matrix(ROW_3), parts(work[...]))
    mine = product(parts(mine), matrix(COLUMN_3))
    work[...] = mine * sign[LAST]
    trade_bits(work, trades)
    store_matrix(out, work[...])


def call(kernel, in_spaces, out_shapes, scratch, flops):
    specs = [pl.BlockSpec(memory_space=space) for space in in_spaces]
    outs = [jax.ShapeDtypeStruct(shape, dtype) for shape, dtype, _ in out_shapes]
    out_specs = [pl.BlockSpec(memory_space=space) for _, _, space in out_shapes]
    return pl.pallas_call(
        kernel,
        in_specs=specs,
        out_shape=outs,
        out_specs=out_specs,
        scratch_shapes=scratch,
        compiler_params=pltpu.CompilerParams(vmem_limit_bytes=40 * 1024 * 1024),
        cost_estimate=pl.CostEstimate(flops=flops, bytes_accessed=4_000_000, transcendentals=0),
    )


def shards(initial_state, angles, pairings):
    V, S = pltpu.VMEM, pltpu.SMEM
    devices = lax.axis_size("wide") * lax.axis_size("narrow")
    chips = [list(range(core, devices, 2)) for core in range(2)]
    rows = 2 * SIDE
    flat = ((rows, LANES), jnp.float32, V)
    work = [pltpu.VMEM((SIDE, SIDE), jnp.float32)]
    product_flops = 3 * 2 * SIDE**3

    def across(value):
        value = value.reshape(SIDE, SIDE)
        value = lax.all_to_all(value, AXES, 0, 0, tiled=True, axis_index_groups=chips)
        return value.reshape(rows, LANES)

    def beside(value):
        return lax.ppermute(value, AXES, [(d, d ^ 1) for d in range(devices)])

    state = initial_state.reshape(rows, LANES)
    (state,) = call(first_kernel, [S, S, V], [flat], work, 2 * product_flops)(
        angles, pairings, state
    )
    state = across(state)
    high, low, sign, coefficients, flag = call(
        prepare_kernel,
        [S, S],
        [
            ((7, SIDE, SIDE), jnp.bfloat16, V),
            ((7, SIDE, SIDE), jnp.bfloat16, V),
            ((7, SIDE, SIDE), jnp.float32, V),
            ((16, LANES), jnp.float32, V),
            ((1,), jnp.int32, S),
        ],
        [pltpu.SMEM((25,), jnp.int32)],
        product_flops,
    )(angles, pairings)
    (state,) = call(second_kernel, [S, V, V, V, V, V, V], [flat], work, 7 * product_flops)(
        flag, state, beside(state), high, low, sign, coefficients
    )
    state = across(state)
    other = lax.cond(flag[0] == 1, beside, lambda value: value, state)
    (state,) = call(third_kernel, [S, S, V, V, V, V, V, V], [flat], work, 3 * product_flops)(
        pairings, flag, state, other, high, low, sign, coefficients
    )
    return state.reshape(-1)


def solution(mesh):
    return jax.shard_map(
        shards,
        mesh=mesh,
        in_specs=(P(AXES), P(), P()),
        out_specs=P(AXES),
        check_vma=False,
    )
```

```python
import jax
import jax.numpy as jnp
from jax import lax
from jax.experimental import pallas as pl
from jax.experimental.pallas import tpu as pltpu
from jax.sharding import PartitionSpec as P

SIDE = 256
LANES = 128
LOCAL = 16
PAIRS = 12
AXES = ("wide", "narrow")
LANE_PLACES = list(range(7))
ROW_PLACES = list(range(7, 15))
HALF = 15
DEVICE_ROWS = list(range(16, 24))
DEVICE_HALF = 24


def from_partner(block, axis, bit):
    count = lax.axis_size(axis)
    route = []
    for low in range(count):
        high = low | 1 << bit
        if high != low and high < count:
            route += [(low, high), (high, low)]
    return lax.ppermute(block, axis, route)


def kron_rotation(angle_list):
    matrix = jnp.ones((1, 1), jnp.float32)
    for angle_value in angle_list:
        cosine = jnp.cos(angle_value / 2)
        sine_half = jnp.sin(angle_value / 2)
        single = jnp.stack([jnp.stack([cosine, -sine_half]), jnp.stack([sine_half, cosine])])
        matrix = jnp.kron(single, matrix)
    return matrix


def rotate_bits(amplitudes, layer_angles, bit_low, qubit_low, bit_count):
    amp_count = amplitudes.shape[0]
    for offset in range(0, bit_count, 7):
        group_bits = min(7, bit_count - offset)
        matrix = kron_rotation(
            [layer_angles[qubit_low + offset + member] for member in range(group_bits)]
        )
        group_size = 2**group_bits
        inner_size = 2 ** (bit_low + offset)
        outer_size = amp_count // (group_size * inner_size)
        if inner_size == 1:
            blocks = amplitudes.reshape(outer_size, group_size)
            amplitudes = jnp.dot(blocks, matrix.T, precision=lax.Precision.HIGHEST).reshape(
                amp_count
            )
        else:
            blocks = amplitudes.reshape(outer_size, group_size, inner_size)
            amplitudes = jnp.einsum(
                "ij,ajb->aib", matrix, blocks, precision=lax.Precision.HIGHEST
            ).reshape(amp_count)
    return amplitudes


def entangle(amplitudes, pair_row, positions):
    pair_count = pair_row.shape[0] // 2
    first_qubits = pair_row[0 : 2 * pair_count : 2]
    second_qubits = pair_row[1 : 2 * pair_count : 2]
    joint_bits = (
        jnp.right_shift(positions[None, :], first_qubits[:, None])
        & jnp.right_shift(positions[None, :], second_qubits[:, None])
        & 1
    )
    parity = jnp.sum(joint_bits, axis=0) % 2
    return jnp.where(parity == 1, -amplitudes, amplitudes)


def remap_narrow(arranged):
    return lax.all_to_all(arranged, "narrow", split_axis=1, concat_axis=1, tiled=True)


def plain_circuit(initial_state, angles, pairings):
    amplitudes = initial_state
    amp_count = amplitudes.shape[0]
    local_bits = amp_count.bit_length() - 1
    wide_size = lax.axis_size("wide")
    narrow_size = lax.axis_size("narrow")
    wide_bits = wide_size.bit_length() - 1
    narrow_bits = narrow_size.bit_length() - 1
    device_bits = wide_bits + narrow_bits
    low_bits = local_bits - device_bits
    wide_index = lax.axis_index("wide")
    device_number = wide_index * narrow_size + lax.axis_index("narrow")
    local_index = jnp.arange(amp_count, dtype=jnp.int32)
    plain_positions = device_number * amp_count + local_index
    for layer_number in range(angles.shape[0]):
        layer_angles = angles[layer_number]
        amplitudes = rotate_bits(amplitudes, layer_angles, 0, 0, local_bits)
        arranged = remap_narrow(amplitudes.reshape(wide_size, narrow_size, -1))
        moved = rotate_bits(
            arranged.reshape(amp_count), layer_angles, low_bits, local_bits, narrow_bits
        )
        amplitudes = remap_narrow(moved.reshape(wide_size, narrow_size, -1)).reshape(amp_count)
        for wide_bit in range(wide_bits):
            partner = from_partner(amplitudes, "wide", wide_bit)
            angle_value = layer_angles[local_bits + narrow_bits + wide_bit]
            cosine = jnp.cos(angle_value / 2)
            sine_half = jnp.sin(angle_value / 2)
            upper_bit = jnp.right_shift(wide_index, wide_bit) & 1
            factor = jnp.where(upper_bit == 1, sine_half, -sine_half)
            amplitudes = cosine * amplitudes + factor * partner
        amplitudes = entangle(amplitudes, pairings[layer_number], plain_positions)
    return amplitudes


def trig(angle):
    t = angle * 0.5
    u = t * t
    sine = 1.0 / 6227020800
    for term in (-1.0 / 39916800, 1.0 / 362880, -1.0 / 5040, 1.0 / 120, -1.0 / 6, 1.0):
        sine = sine * u + term
    cosine = -1.0 / 87178291200
    for term in (1.0 / 479001600, -1.0 / 3628800, 1.0 / 40320, -1.0 / 720, 1.0 / 24, -0.5, 1.0):
        cosine = cosine * u + term
    return cosine, sine * t


def iota(shape, axis):
    return lax.broadcasted_iota(jnp.int32, shape, axis)


def outside_partners(pairings, layer):
    mask = jnp.int32(0)
    one = jnp.int32(1)
    for k in range(PAIRS):
        p, r = pairings[layer, 2 * k], pairings[layer, 2 * k + 1]
        mask = mask | jnp.where(p >= LOCAL, lax.shift_left(one, r), 0)
        mask = mask | jnp.where(r >= LOCAL, lax.shift_left(one, p), 0)
    return mask


def choose_trades(bound):
    free = ~bound & 127
    failed = jnp.int32(0)
    trades = []
    for place in range(7, 16):
        wanted = (bound >> place) & 1
        taken = jnp.where(wanted == 1, free & -free, 0)
        failed = failed | jnp.where(taken == 0, wanted, 0)
        free = free & ~taken
        trades.append(taken)
    return trades, failed


def qubits_at(trades):
    table = []
    for lane in range(7):
        held = jnp.int32(lane)
        for place in range(7, 16):
            held = jnp.where(trades[place - 7] == 1 << lane, place, held)
        table.append(held)
    for place in range(7, 16):
        taken = trades[place - 7]
        held = jnp.int32(0)
        for lane in range(1, 7):
            held = held + jnp.where(taken >= 1 << lane, 1, 0)
        table.append(jnp.where(taken == 0, place, held))
    return table


def angle_table(entries):
    spot = iota((8, LANES), 0) * LANES + iota((8, LANES), 1)
    table = jnp.zeros((8, LANES), jnp.float32)
    for row, lane, value in entries:
        table = jnp.where(spot == row * LANES + lane, value, table)
    return table


def bit_masks():
    i, j = iota((LANES, LANES), 0), iota((LANES, LANES), 1)
    same = [((i ^ j) >> b) & 1 == 0 for b in range(7)]
    upper = [(i >> b) & 1 == 1 for b in range(7)]
    return same, upper


def kron_matrix(masks, turns, row, places, transposed):
    same, upper = masks
    cosines, sines = turns

    def turn(place):
        c = cosines[row : row + 1, place : place + 1]
        s = sines[row : row + 1, place : place + 1]
        return c, -s if transposed else s

    total = None
    for b in range(7):
        c, s = turn(places[b])
        factor = jnp.where(same[b], c, jnp.where(upper[b], s, -s))
        total = factor if total is None else total * factor
    c, s = turn(places[7])
    top = jnp.concatenate([total * c, total * -s], axis=1)
    low = jnp.concatenate([total * s, total * c], axis=1)
    return parts(jnp.concatenate([top, low], axis=0))


def parts(value):
    high = value.astype(jnp.bfloat16)
    low = (value - high.astype(jnp.float32)).astype(jnp.bfloat16)
    return high, low


def product(left, right):
    (lh, ll), (rh, rl) = left, right

    def dot(a, b):
        return jnp.dot(a, b, preferred_element_type=jnp.float32)

    return dot(lh, rh) + (dot(lh, rl) + dot(ll, rh))


def on_rows(matrix, value):
    return product(matrix, parts(value))


def on_columns(value, matrix):
    return product(parts(value), matrix)


def turn_halves(turns, row, place, value):
    cosines, sines = turns
    c = cosines[row : row + 1, place : place + 1]
    s = sines[row : row + 1, place : place + 1]
    first, second = value[:, :LANES], value[:, LANES:]
    return jnp.concatenate([c * first - s * second, s * first + c * second], axis=1)


def load_matrix(ref):
    return jnp.concatenate([ref[:SIDE, :], ref[SIDE:, :]], axis=1)


def store_matrix(ref, value):
    ref[:SIDE, :] = value[:, :LANES]
    ref[SIDE:, :] = value[:, LANES:]


def sign_array(pairs, keep, device=None):
    def shifts(shape, axis):
        spot = iota(shape, axis)
        p = jnp.full(shape, -1, jnp.int32)
        r = p
        for k, (first, second) in enumerate(pairs):
            p = jnp.where(spot == k, first, p)
            r = jnp.where(spot == k, second, r)
        applies = jnp.where((p >= 0) & keep(p, r), 1, 0)
        if device is not None:
            held = jnp.full(shape, device, jnp.int32)
            for place in (p, r):
                bit = lax.shift_right_logical(held, jnp.maximum(place - LOCAL, 0)) & 1
                applies = applies & jnp.where(place >= LOCAL, bit, 1)
        return p, r, applies

    def row_bit(place, applies):
        inside = (place >= 7) & (place < HALF)
        return jnp.where(applies == 1, jnp.where(inside, place - 7, 8), 31)

    def column_bit(place):
        return jnp.where(place < 7, place, jnp.where(place == HALF, 7, 8))

    p, r, applies = shifts((1, 16), 1)
    row = iota((SIDE, 16), 0) | SIDE
    row = lax.shift_right_logical(row, jnp.broadcast_to(row_bit(p, applies), row.shape)) & (
        lax.shift_right_logical(row, jnp.broadcast_to(row_bit(r, applies), row.shape))
    )
    p, r, _ = shifts((16, 1), 0)
    column = iota((16, SIDE), 1) | SIDE
    column = lax.shift_right_logical(column, jnp.broadcast_to(column_bit(p), column.shape)) & (
        lax.shift_right_logical(column, jnp.broadcast_to(column_bit(r), column.shape))
    )
    count = jnp.dot(
        (row & 1).astype(jnp.float32).astype(jnp.bfloat16),
        (column & 1).astype(jnp.float32).astype(jnp.bfloat16),
        preferred_element_type=jnp.float32,
    )
    return (1 - 2 * (count.astype(jnp.int32) & 1)).astype(jnp.float32)


def has_device(p, r):
    return (p >= LOCAL) | (r >= LOCAL)


def all_local(p, r):
    return (p < LOCAL) & (r < LOCAL)


def trade_bits(work, trades):
    lane = iota((SIDE, LANES), 1)
    row = iota((SIDE, LANES), 0)
    for bit in range(8):
        taken = trades[bit]
        step = 1 << bit

        @pl.when(taken != 0)
        def _():
            lane_up = (lane & taken) != 0
            row_up = (row & step) != 0
            for half in range(2):
                columns = slice(half * LANES, half * LANES + LANES)
                held = work[:, columns]
                from_later = pltpu.roll(pltpu.roll(held, SIDE - step, 0), taken, 1)
                from_sooner = pltpu.roll(pltpu.roll(held, step, 0), LANES - taken, 1)
                moved = jnp.where(lane_up, from_later, from_sooner)
                work[:, columns] = jnp.where(row_up == lane_up, held, moved)

    taken = trades[8]

    @pl.when(taken != 0)
    def _():
        lane_up = (lane & taken) != 0
        first = work[:, :LANES]
        second = work[:, LANES:]
        work[:, :LANES] = jnp.where(lane_up, pltpu.roll(second, taken, 1), first)
        work[:, LANES:] = jnp.where(lane_up, second, pltpu.roll(first, LANES - taken, 1))


def first_kernel(angles_in, pairings_in, state_in, out, plan, work, state, angles, pairings, arrived):
    copies = [
        pltpu.make_async_copy(source, target, arrived.at[slot])
        for slot, (source, target) in enumerate(
            ((angles_in, angles), (pairings_in, pairings), (state_in, state))
        )
    ]
    for copy in copies:
        copy.start()
    copies[0].wait()
    copies[1].wait()
    apart = outside_partners(pairings, 0)
    trades, failed = choose_trades(apart & outside_partners(pairings, 1))
    plan[0] = failed
    for bit in range(9):
        plan[1 + bit] = trades[bit]
    plan[10] = apart
    entries = [(0, q, angles[0, q]) for q in range(LOCAL)]
    entries += [(1, q, jnp.where((apart >> q) & 1 == 1, 0.0, angles[1, q])) for q in range(LOCAL)]
    turns = trig(angle_table(entries))
    masks = bit_masks()
    matrices = [
        (
            kron_matrix(masks, turns, layer, ROW_PLACES, False),
            kron_matrix(masks, turns, layer, LANE_PLACES + [HALF], True),
        )
        for layer in range(2)
    ]
    pairs = [(pairings[0, 2 * k], pairings[0, 2 * k + 1]) for k in range(PAIRS)]
    sign = sign_array(pairs, all_local)
    copies[2].wait()
    value = load_matrix(state)
    value = on_columns(on_rows(matrices[0][0], value), matrices[0][1]) * sign
    work[...] = on_columns(on_rows(matrices[1][0], value), matrices[1][1])
    trade_bits(work, trades)
    store_matrix(out, work[...])


DEVICE_1, DEVICE_2, DEVICE_3, COLUMN_2, ROW_2, ROW_3, COLUMN_3 = range(7)
SIGN_1, SIGN_2, SIGN_LATE, SIGN_3 = range(4)


def prepare_kernel(angles, pairings, plan, high, low, sign, table, places):
    trades = [plan[1 + bit] for bit in range(9)]
    apart = plan[10]
    held = qubits_at(trades)
    for place in range(LOCAL):
        places[place] = held[place]
    for place in range(LOCAL, 25):
        places[place] = jnp.int32(place)
    entries = [(0, p, angles[0, p]) for p in range(LOCAL, 25)]
    entries += [(1, p, angles[1, p]) for p in range(LOCAL, 25)]
    entries += [(2, p, angles[2, p]) for p in range(LOCAL, 25)]
    for p in range(LOCAL):
        late = lax.shift_right_logical(apart, held[p]) & 1
        entries.append((1, p, jnp.where(late == 1, angles[1, held[p]], 0.0)))
        entries.append((2, p, angles[2, held[p]]))
    turns = trig(angle_table(entries))
    table[0:8, :], table[8:16, :] = turns
    masks = bit_masks()
    for slot, layer, spots, transposed in (
        (DEVICE_1, 0, DEVICE_ROWS, False),
        (DEVICE_2, 1, DEVICE_ROWS, False),
        (DEVICE_3, 2, DEVICE_ROWS, False),
        (COLUMN_2, 1, LANE_PLACES + [DEVICE_HALF], True),
        (ROW_2, 1, ROW_PLACES, False),
        (ROW_3, 2, ROW_PLACES, False),
        (COLUMN_3, 2, LANE_PLACES + [HALF], True),
    ):
        high[slot], low[slot] = kron_matrix(masks, turns, layer, spots, transposed)
    device = lax.axis_index("wide") * lax.axis_size("narrow") + lax.axis_index("narrow")

    def pairs_of(layer, inner):
        pairs = []
        for k in range(2 * PAIRS):
            place = places[pairings[layer, k]]
            if inner:
                moved = jnp.where(place >= LOCAL, place - 9, place + 9)
                place = jnp.where(place < 7, place, moved)
            pairs.append(place)
        return list(zip(pairs[::2], pairs[1::2]))

    def has_rows(p, r):
        return ((p >= 7) & (p < LOCAL)) | ((r >= 7) & (r < LOCAL))

    sign[SIGN_1] = sign_array(pairs_of(0, True), has_rows, device)
    sign[SIGN_2] = sign_array(pairs_of(1, True), has_rows, device)
    sign[SIGN_LATE] = sign_array(pairs_of(1, False), all_local)
    sign[SIGN_3] = sign_array(pairs_of(2, False), lambda p, r: p == p, device)


def second_kernel(state, high, low, sign, table, out):
    def matrix(slot):
        return high[slot], low[slot]

    turns = table[0:8, :], table[8:16, :]
    value = on_rows(matrix(DEVICE_1), load_matrix(state))
    value = turn_halves(turns, 0, DEVICE_HALF, value) * sign[SIGN_1]
    value = on_columns(on_rows(matrix(DEVICE_2), value), matrix(COLUMN_2)) * sign[SIGN_2]
    value = on_rows(matrix(DEVICE_3), value)
    store_matrix(out, turn_halves(turns, 2, DEVICE_HALF, value))


def third_kernel(plan, high, low, sign, table, state, out, work):
    def matrix(slot):
        return high[slot], low[slot]

    trades = [plan[1 + bit] for bit in range(9)]
    turns = table[0:8, :], table[8:16, :]
    value = on_rows(matrix(ROW_2), load_matrix(state))
    value = turn_halves(turns, 1, HALF, value) * sign[SIGN_LATE]
    value = on_columns(on_rows(matrix(ROW_3), value), matrix(COLUMN_3))
    work[...] = value * sign[SIGN_3]
    trade_bits(work, trades)
    store_matrix(out, work[...])


def call(kernel, in_spaces, out_shapes, scratch, flops, limit):
    specs = [pl.BlockSpec(memory_space=space) for space in in_spaces]
    outs = [jax.ShapeDtypeStruct(shape, dtype) for shape, dtype, _ in out_shapes]
    out_specs = [pl.BlockSpec(memory_space=space) for _, _, space in out_shapes]
    return pl.pallas_call(
        kernel,
        in_specs=specs,
        out_shape=outs,
        out_specs=out_specs,
        scratch_shapes=scratch,
        compiler_params=pltpu.CompilerParams(vmem_limit_bytes=limit * 1024 * 1024),
        cost_estimate=pl.CostEstimate(flops=flops, bytes_accessed=4_000_000, transcendentals=0),
    )


def shards(initial_state, angles, pairings):
    V, S = pltpu.VMEM, pltpu.SMEM
    rows = 2 * SIDE
    flat = ((rows, LANES), jnp.float32, V)
    work = [pltpu.VMEM((SIDE, SIDE), jnp.float32)]
    product_flops = 3 * 2 * SIDE**3

    def across(value):
        return lax.all_to_all(value, AXES, 0, 0, tiled=True)

    fetched = [
        pltpu.VMEM((rows, LANES), jnp.float32),
        pltpu.SMEM(angles.shape, jnp.float32),
        pltpu.SMEM(pairings.shape, jnp.int32),
        pltpu.SemaphoreType.DMA((3,)),
    ]
    state, plan = call(
        first_kernel,
        [pltpu.HBM] * 3,
        [flat, ((16,), jnp.int32, S)],
        work + fetched,
        4 * product_flops,
        60,
    )(angles, pairings, initial_state.reshape(rows, LANES))
    state = across(state)
    prepared = call(
        prepare_kernel,
        [S, S, S],
        [
            ((7, SIDE, SIDE), jnp.bfloat16, V),
            ((7, SIDE, SIDE), jnp.bfloat16, V),
            ((4, SIDE, SIDE), jnp.float32, V),
            ((16, LANES), jnp.float32, V),
        ],
        [pltpu.SMEM((25,), jnp.int32)],
        40 * product_flops,
        32,
    )(angles, pairings, plan)
    failed = plan[0] == 1
    state, failed, prepared = lax.optimization_barrier((state, failed, prepared))
    (state,) = call(second_kernel, [V] * 5, [flat], [], 4 * product_flops, 32)(state, *prepared)
    state = across(state)

    def finish(value):
        (last,) = call(third_kernel, [S] + [V] * 5, [flat], work, 3 * product_flops, 32)(
            plan, *prepared, value
        )
        return last.reshape(-1)

    def start_over(value):
        return plain_circuit(initial_state, angles, pairings)

    return lax.cond(failed, start_over, finish, state)


def solution(mesh):
    return jax.shard_map(
        shards,
        mesh=mesh,
        in_specs=(P(AXES), P(), P()),
        out_specs=P(AXES),
        check_vma=False,
    )
```

```python
import functools

import jax
import jax.numpy as jnp
from jax import lax
from jax.experimental import pallas as pl
from jax.experimental.pallas import tpu as pltpu
from jax.sharding import PartitionSpec as P

SIDE = 256
LANES = 128
LOCAL = 16
PAIRS = 12
AXES = ("wide", "narrow")
LANE_PLACES = list(range(7))
ROW_PLACES = list(range(7, 15))
HALF = 15
DEVICE_ROWS = list(range(16, 24))
DEVICE_HALF = 24


def trig(angle):
    t = angle * 0.5
    u = t * t
    sine = 1.0 / 6227020800
    for term in (-1.0 / 39916800, 1.0 / 362880, -1.0 / 5040, 1.0 / 120, -1.0 / 6, 1.0):
        sine = sine * u + term
    cosine = -1.0 / 87178291200
    for term in (1.0 / 479001600, -1.0 / 3628800, 1.0 / 40320, -1.0 / 720, 1.0 / 24, -0.5, 1.0):
        cosine = cosine * u + term
    return cosine, sine * t


def iota(shape, axis):
    return lax.broadcasted_iota(jnp.int32, shape, axis)


def choose_trades(bound):
    free = ~bound & 127
    stuck = jnp.int32(0)
    trades = []
    for place in range(7, 16):
        wanted = bound & (1 << place)
        taken = jnp.where(wanted != 0, free & -free, 0)
        stuck = stuck | jnp.where(taken == 0, wanted, 0)
        free = free & ~taken
        trades.append(taken)
    return trades, stuck


def partners_of(pairings, layer, mask):
    found = jnp.int32(0)
    one = jnp.int32(1)
    for k in range(PAIRS):
        p, r = pairings[layer, 2 * k], pairings[layer, 2 * k + 1]
        found = found | lax.shift_left(lax.shift_right_logical(mask, r) & one, p)
        found = found | lax.shift_left(lax.shift_right_logical(mask, p) & one, r)
    return found


def qubits_at(trades):
    table = []
    for lane in range(7):
        held = jnp.int32(lane)
        for place in range(7, 16):
            held = jnp.where(trades[place - 7] == 1 << lane, place, held)
        table.append(held)
    for place in range(7, 16):
        taken = trades[place - 7]
        held = jnp.int32(0)
        for lane in range(1, 7):
            held = held + jnp.where(taken >= 1 << lane, 1, 0)
        table.append(jnp.where(taken == 0, place, held))
    return table


def angle_table(entries):
    spot = iota((8, LANES), 0) * LANES + iota((8, LANES), 1)
    table = jnp.zeros((8, LANES), jnp.float32)
    for row, lane, value in entries:
        table = jnp.where(spot == row * LANES + lane, value, table)
    return table


def bit_masks():
    i, j = iota((LANES, LANES), 0), iota((LANES, LANES), 1)
    same = [((i ^ j) >> b) & 1 == 0 for b in range(7)]
    upper = [(i >> b) & 1 == 1 for b in range(7)]
    return same, upper


def kron_matrix(masks, turns, row, places, transposed):
    same, upper = masks
    cosines, sines = turns

    def turn(place):
        c = cosines[row : row + 1, place : place + 1]
        s = sines[row : row + 1, place : place + 1]
        return c, -s if transposed else s

    total = None
    for b in range(7):
        c, s = turn(places[b])
        factor = jnp.where(same[b], c, jnp.where(upper[b], s, -s))
        total = factor if total is None else total * factor
    c, s = turn(places[7])
    top = jnp.concatenate([total * c, total * -s], axis=1)
    low = jnp.concatenate([total * s, total * c], axis=1)
    return parts(jnp.concatenate([top, low], axis=0))


def parts(value):
    high = value.astype(jnp.bfloat16)
    low = (value - high.astype(jnp.float32)).astype(jnp.bfloat16)
    return high, low


def product(left, right):
    (lh, ll), (rh, rl) = left, right

    def dot(a, b):
        return jnp.dot(a, b, preferred_element_type=jnp.float32)

    return dot(lh, rh) + (dot(lh, rl) + dot(ll, rh))


def on_rows(matrix, value):
    return product(matrix, parts(value))


def on_columns(value, matrix):
    return product(parts(value), matrix)


def turn_halves(turns, row, place, value):
    cosines, sines = turns
    c = cosines[row : row + 1, place : place + 1]
    s = sines[row : row + 1, place : place + 1]
    first, second = value[:, :LANES], value[:, LANES:]
    return jnp.concatenate([c * first - s * second, s * first + c * second], axis=1)


def load_matrix(ref):
    return jnp.concatenate([ref[:SIDE, :], ref[SIDE:, :]], axis=1)


def store_matrix(ref, value):
    ref[:SIDE, :] = value[:, :LANES]
    ref[SIDE:, :] = value[:, LANES:]


def sign_array(pairs, keep, device=None):
    def shifts(shape, axis):
        spot = iota(shape, axis)
        p = jnp.full(shape, -1, jnp.int32)
        r = p
        for k, (first, second) in enumerate(pairs):
            p = jnp.where(spot == k, first, p)
            r = jnp.where(spot == k, second, r)
        applies = jnp.where((p >= 0) & keep(p, r), 1, 0)
        if device is not None:
            held = jnp.full(shape, device, jnp.int32)
            for place in (p, r):
                bit = lax.shift_right_logical(held, jnp.maximum(place - LOCAL, 0)) & 1
                applies = applies & jnp.where(place >= LOCAL, bit, 1)
        return p, r, applies

    def row_bit(place, applies):
        inside = (place >= 7) & (place < HALF)
        return jnp.where(applies == 1, jnp.where(inside, place - 7, 8), 31)

    def column_bit(place):
        return jnp.where(place < 7, place, jnp.where(place == HALF, 7, 8))

    p, r, applies = shifts((1, 16), 1)
    row = iota((SIDE, 16), 0) | SIDE
    row = lax.shift_right_logical(row, jnp.broadcast_to(row_bit(p, applies), row.shape)) & (
        lax.shift_right_logical(row, jnp.broadcast_to(row_bit(r, applies), row.shape))
    )
    p, r, _ = shifts((16, 1), 0)
    column = iota((16, SIDE), 1) | SIDE
    column = lax.shift_right_logical(column, jnp.broadcast_to(column_bit(p), column.shape)) & (
        lax.shift_right_logical(column, jnp.broadcast_to(column_bit(r), column.shape))
    )
    count = jnp.dot(
        (row & 1).astype(jnp.float32).astype(jnp.bfloat16),
        (column & 1).astype(jnp.float32).astype(jnp.bfloat16),
        preferred_element_type=jnp.float32,
    )
    return (1 - 2 * (count.astype(jnp.int32) & 1)).astype(jnp.float32)


def has_device(p, r):
    return (p >= LOCAL) | (r >= LOCAL)


def all_local(p, r):
    return (p < LOCAL) & (r < LOCAL)


def trade_bits(work, trades):
    lane = iota((SIDE, LANES), 1)
    row = iota((SIDE, LANES), 0)
    for bit in range(8):
        taken = trades[bit]
        step = 1 << bit

        @pl.when(taken != 0)
        def _():
            lane_up = (lane & taken) != 0
            row_up = (row & step) != 0
            for half in range(2):
                columns = slice(half * LANES, half * LANES + LANES)
                held = work[:, columns]
                from_later = pltpu.roll(pltpu.roll(held, SIDE - step, 0), taken, 1)
                from_sooner = pltpu.roll(pltpu.roll(held, step, 0), LANES - taken, 1)
                moved = jnp.where(lane_up, from_later, from_sooner)
                work[:, columns] = jnp.where(row_up == lane_up, held, moved)

    taken = trades[8]

    @pl.when(taken != 0)
    def _():
        lane_up = (lane & taken) != 0
        first = work[:, :LANES]
        second = work[:, LANES:]
        work[:, :LANES] = jnp.where(lane_up, pltpu.roll(second, taken, 1), first)
        work[:, LANES:] = jnp.where(lane_up, second, pltpu.roll(first, LANES - taken, 1))


def first_kernel(angles_in, pairings_in, state_in, out, plan, work, state, angles, pairings, arrived):
    copies = [
        pltpu.make_async_copy(source, target, arrived.at[slot])
        for slot, (source, target) in enumerate(
            ((angles_in, angles), (pairings_in, pairings), (state_in, state))
        )
    ]
    for copy in copies:
        copy.start()
    for copy in copies:
        copy.wait()
    of_device = jnp.int32(((1 << 25) - 1) - ((1 << LOCAL) - 1))
    apart = partners_of(pairings, 0, of_device)
    bound = apart & partners_of(pairings, 1, of_device) & ((1 << LOCAL) - 1)
    trades, stuck = choose_trades(bound)
    held = qubits_at(trades)
    plan[0] = stuck
    plan[1] = apart
    for place in range(LOCAL):
        plan[2 + place] = held[place]
    for bit in range(9):
        plan[18 + bit] = trades[bit]
    entries = [(0, q, angles[0, q]) for q in range(LOCAL)]
    for place in range(7, LOCAL):
        late = lax.shift_right_logical(apart, held[place]) & 1
        entries.append((1, place, jnp.where(late == 1, 0.0, angles[1, held[place]])))
    turns = trig(angle_table(entries))
    masks = bit_masks()
    rows = kron_matrix(masks, turns, 0, ROW_PLACES, False)
    columns = kron_matrix(masks, turns, 0, LANE_PLACES + [HALF], True)
    early = kron_matrix(masks, turns, 1, ROW_PLACES, False)
    pairs = [(pairings[0, 2 * k], pairings[0, 2 * k + 1]) for k in range(PAIRS)]
    sign = sign_array(pairs, all_local)
    value = on_columns(on_rows(rows, load_matrix(state)), columns) * sign
    work[...] = value
    trade_bits(work, trades)
    value = on_rows(early, work[...])
    store_matrix(out, turn_halves(turns, 1, HALF, value))


DEVICE_1, DEVICE_2, DEVICE_3, COLUMN_2, ROW_2, ROW_3, COLUMN_3 = range(7)
SIGN_1, SIGN_2, SIGN_LATE, SIGN_3 = range(4)


def prepare_kernel(angles, pairings, plan, high, low, sign, table, places):
    stuck, apart = plan[0], plan[1]
    held = [plan[2 + place] for place in range(LOCAL)]
    waiting = partners_of(pairings, 1, stuck)
    for place in range(LOCAL):
        places[held[place]] = jnp.int32(place)
    for place in range(LOCAL, 25):
        places[place] = jnp.int32(place)
    entries = []
    for p in range(LOCAL, 25):
        waits = (waiting >> p) & 1 == 1
        entries += [(0, p, angles[0, p]), (1, p, angles[1, p])]
        entries.append((2, p, jnp.where(waits, 0.0, angles[2, p])))
        entries.append((3, p, jnp.where(waits, angles[2, p], 0.0)))
    for p in range(7):
        entries += [(1, p, angles[1, held[p]]), (2, p, angles[2, held[p]])]
    for p in range(7, LOCAL):
        late = lax.shift_right_logical(apart, held[p]) & 1
        entries.append((1, p, jnp.where(late == 1, angles[1, held[p]], 0.0)))
        entries.append((2, p, angles[2, held[p]]))
    turns = trig(angle_table(entries))
    table[0:8, :], table[8:16, :] = turns
    masks = bit_masks()
    for slot, layer, spots, transposed in (
        (DEVICE_1, 0, DEVICE_ROWS, False),
        (DEVICE_2, 1, DEVICE_ROWS, False),
        (DEVICE_3, 2, DEVICE_ROWS, False),
        (COLUMN_2, 1, LANE_PLACES + [DEVICE_HALF], True),
        (ROW_2, 1, ROW_PLACES, False),
        (ROW_3, 2, ROW_PLACES, False),
        (COLUMN_3, 2, LANE_PLACES + [HALF], True),
    ):
        high[slot], low[slot] = kron_matrix(masks, turns, layer, spots, transposed)
    device = lax.axis_index("wide") * lax.axis_size("narrow") + lax.axis_index("narrow")

    def pairs_of(layer, inner):
        pairs = []
        for k in range(2 * PAIRS):
            place = places[pairings[layer, k]]
            if inner:
                moved = jnp.where(place >= LOCAL, place - 9, place + 9)
                place = jnp.where(place < 7, place, moved)
            pairs.append(place)
        return list(zip(pairs[::2], pairs[1::2]))

    def is_stuck(place):
        mask = jnp.full(place.shape, stuck, jnp.int32)
        return (lax.shift_right_logical(mask, jnp.maximum(place, 0)) & 1) == 1

    def local_or_stuck(p, r):
        return all_local(p, r) | is_stuck(p) | is_stuck(r)

    def on_device(p, r):
        return ((p >= 7) & (p < LOCAL)) | ((r >= 7) & (r < LOCAL))

    def on_device_not_stuck(p, r):
        return on_device(p, r) & ~(is_stuck(p - 9) | is_stuck(r - 9))

    sign[SIGN_1] = sign_array(pairs_of(0, True), on_device, device)
    sign[SIGN_2] = sign_array(pairs_of(1, True), on_device_not_stuck, device)
    sign[SIGN_LATE] = sign_array(pairs_of(1, False), local_or_stuck, device)
    sign[SIGN_3] = sign_array(pairs_of(2, False), lambda p, r: p == p, device)


def second_kernel(state, high, low, sign, table, out):
    def matrix(slot):
        return high[slot], low[slot]

    turns = table[0:8, :], table[8:16, :]
    value = on_rows(matrix(DEVICE_1), load_matrix(state))
    value = turn_halves(turns, 0, DEVICE_HALF, value) * sign[SIGN_1]
    value = on_columns(on_rows(matrix(DEVICE_2), value), matrix(COLUMN_2)) * sign[SIGN_2]
    value = on_rows(matrix(DEVICE_3), value)
    store_matrix(out, turn_halves(turns, 2, DEVICE_HALF, value))


def third_kernel(front, back, plan, high, low, sign, table, state, out, work):
    def matrix(slot):
        return high[slot], low[slot]

    turns = table[0:8, :], table[8:16, :]
    value = load_matrix(state)
    if front:
        value = on_rows(matrix(ROW_2), value)
        value = turn_halves(turns, 1, HALF, value) * sign[SIGN_LATE]
        value = on_columns(on_rows(matrix(ROW_3), value), matrix(COLUMN_3))
    if back:
        work[...] = value * sign[SIGN_3]
        trade_bits(work, [plan[18 + bit] for bit in range(9)])
        value = work[...]
    store_matrix(out, value)


def call(kernel, in_spaces, out_shapes, scratch, flops, limit):
    specs = [pl.BlockSpec(memory_space=space) for space in in_spaces]
    outs = [jax.ShapeDtypeStruct(shape, dtype) for shape, dtype, _ in out_shapes]
    out_specs = [pl.BlockSpec(memory_space=space) for _, _, space in out_shapes]
    return pl.pallas_call(
        kernel,
        in_specs=specs,
        out_shape=outs,
        out_specs=out_specs,
        scratch_shapes=scratch,
        compiler_params=pltpu.CompilerParams(vmem_limit_bytes=limit * 1024 * 1024),
        cost_estimate=pl.CostEstimate(flops=flops, bytes_accessed=4_000_000, transcendentals=0),
    )


def shards(initial_state, angles, pairings):
    V, S = pltpu.VMEM, pltpu.SMEM
    rows = 2 * SIDE
    flat = ((rows, LANES), jnp.float32, V)
    work = [pltpu.VMEM((SIDE, SIDE), jnp.float32)]
    product_flops = 3 * 2 * SIDE**3

    def across(value):
        return lax.all_to_all(value, AXES, 0, 0, tiled=True)

    fetched = [
        pltpu.VMEM((rows, LANES), jnp.float32),
        pltpu.SMEM(angles.shape, jnp.float32),
        pltpu.SMEM(pairings.shape, jnp.int32),
        pltpu.SemaphoreType.DMA((3,)),
    ]
    state, plan = call(
        first_kernel,
        [pltpu.HBM] * 3,
        [flat, ((27,), jnp.int32, S)],
        work + fetched,
        3 * product_flops,
        60,
    )(angles, pairings, initial_state.reshape(rows, LANES))
    state = across(state)
    prepared = call(
        prepare_kernel,
        [S, S, S],
        [
            ((7, SIDE, SIDE), jnp.bfloat16, V),
            ((7, SIDE, SIDE), jnp.bfloat16, V),
            ((4, SIDE, SIDE), jnp.float32, V),
            ((16, LANES), jnp.float32, V),
        ],
        [pltpu.SMEM((25,), jnp.int32)],
        40 * product_flops,
        32,
    )(angles, pairings, plan)
    stuck = plan[0] != 0
    state, stuck, prepared = lax.optimization_barrier((state, stuck, prepared))
    (state,) = call(second_kernel, [V] * 5, [flat], [], 4 * product_flops, 32)(state, *prepared)
    state = across(state)

    def third(value, front, back):
        kernel = functools.partial(third_kernel, front, back)
        return call(kernel, [S] + [V] * 5, [flat], work, 3 * product_flops, 32)(
            plan, *prepared, value
        )[0]

    def finish(value):
        return third(value, True, True).reshape(-1)

    def finish_slowly(value):
        value = third(value, True, False)
        table = prepared[3]
        device = lax.axis_index(AXES)
        devices = lax.axis_size(AXES)
        for bit in range(9):
            route = [(d, d ^ 1 << bit) for d in range(devices)]
            other = lax.ppermute(value, AXES, route)
            c, s = table[3, LOCAL + bit], table[11, LOCAL + bit]
            upper = lax.shift_right_logical(device, bit) & 1 == 1
            value = c * value + jnp.where(upper, s, -s) * other
        return third(value, False, True).reshape(-1)

    return lax.cond(stuck, finish_slowly, finish, state)


def solution(mesh):
    return jax.shard_map(
        shards,
        mesh=mesh,
        in_specs=(P(AXES), P(), P()),
        out_specs=P(AXES),
        check_vma=False,
    )
```

```python
import functools

import jax
import jax.numpy as jnp
from jax import lax
from jax.experimental import pallas as pl
from jax.experimental.pallas import tpu as pltpu
from jax.sharding import PartitionSpec as P

SIDE = 256
LANES = 128
LOCAL = 16
CORE = 16
SIGNED_CORE = 25
PAIRS = 12
FLIP = 0b10101000
AXES = ("wide", "narrow")
LANE_PLACES = list(range(7))
ROW_PLACES = list(range(7, 15))
HALF = 15
CHIP_PLACES = list(range(17, 25))


def trig(angle):
    t = angle * 0.5
    u = t * t
    sine = 1.0 / 6227020800
    for term in (-1.0 / 39916800, 1.0 / 362880, -1.0 / 5040, 1.0 / 120, -1.0 / 6, 1.0):
        sine = sine * u + term
    cosine = -1.0 / 87178291200
    for term in (1.0 / 479001600, -1.0 / 3628800, 1.0 / 40320, -1.0 / 720, 1.0 / 24, -0.5, 1.0):
        cosine = cosine * u + term
    return cosine, sine * t


def iota(shape, axis):
    return lax.broadcasted_iota(jnp.int32, shape, axis)


def choose_trades(bound):
    free = (~bound & 127) | (lax.shift_right_logical(~bound, HALF) & 1) * LANES
    stuck = jnp.int32(0)
    trades = []
    for place in ROW_PLACES:
        wanted = bound & (1 << place)
        taken = jnp.where(wanted != 0, free & -free, 0)
        stuck = stuck | jnp.where(taken == 0, wanted, 0)
        free = free & ~taken
        trades.append(taken)
    return trades, stuck


def partners_of(pairings, layer, mask):
    found = jnp.int32(0)
    one = jnp.int32(1)
    for k in range(PAIRS):
        p, r = pairings[layer, 2 * k], pairings[layer, 2 * k + 1]
        found = found | lax.shift_left(lax.shift_right_logical(mask, r) & one, p)
        found = found | lax.shift_left(lax.shift_right_logical(mask, p) & one, r)
    return found


def qubits_at(trades):
    table = [jnp.int32(place) for place in range(LOCAL)]
    for lane in range(8):
        own = HALF if lane == 7 else lane
        for place in ROW_PLACES:
            table[own] = jnp.where(trades[place - 7] == 1 << lane, place, table[own])
            table[place] = jnp.where(trades[place - 7] == 1 << lane, own, table[place])
    return table


def angle_table(entries):
    spot = iota((8, LANES), 0) * LANES + iota((8, LANES), 1)
    table = jnp.zeros((8, LANES), jnp.float32)
    for row, lane, value in entries:
        table = jnp.where(spot == row * LANES + lane, value, table)
    return table


def bit_masks():
    i, j = iota((LANES, LANES), 0), iota((LANES, LANES), 1)
    same = [((i ^ j) >> b) & 1 == 0 for b in range(7)]
    upper = [(i >> b) & 1 == 1 for b in range(7)]
    return same, upper


def kron_matrix(masks, turns, row, places, transposed):
    same, upper = masks
    cosines, sines = turns

    def turn(place):
        c = cosines[row : row + 1, place : place + 1]
        s = sines[row : row + 1, place : place + 1]
        return c, -s if transposed else s

    total = None
    for b in range(7):
        c, s = turn(places[b])
        factor = jnp.where(same[b], c, jnp.where(upper[b], s, -s))
        total = factor if total is None else total * factor
    c, s = turn(places[7])
    top = jnp.concatenate([total * c, total * -s], axis=1)
    low = jnp.concatenate([total * s, total * c], axis=1)
    return parts(jnp.concatenate([top, low], axis=0))


def parts(value):
    high = value.astype(jnp.bfloat16)
    low = (value - high.astype(jnp.float32)).astype(jnp.bfloat16)
    return high, low


def product(left, right):
    (lh, ll), (rh, rl) = left, right
    a = jnp.concatenate([lh, lh, ll], axis=1)
    b = jnp.concatenate([rh, rl, rh], axis=0)
    return jnp.dot(a, b, preferred_element_type=jnp.float32)


def on_rows(matrix, value):
    return product(matrix, parts(value))


def on_columns(value, matrix):
    return product(parts(value), matrix)


def load_matrix(ref):
    return jnp.concatenate([ref[:SIDE, :], ref[SIDE:, :]], axis=1)


def store_matrix(ref, value):
    ref[:SIDE, :] = value[:, :LANES]
    ref[SIDE:, :] = value[:, LANES:]


def load_pieces(ref):
    first, second = pl.ds(0, SIDE, stride=2), pl.ds(1, SIDE, stride=2)
    return jnp.concatenate([ref[first, :], ref[second, :]], axis=1)


def store_pieces(ref, value):
    ref[pl.ds(0, SIDE, stride=2), :] = value[:, :LANES]
    ref[pl.ds(1, SIDE, stride=2), :] = value[:, LANES:]


def sign_array(pairs, keep, device=None, swapped=False):
    def shifts(shape, axis):
        spot = iota(shape, axis)
        p = jnp.full(shape, -1, jnp.int32)
        r = p
        for k, (first, second) in enumerate(pairs):
            p = jnp.where(spot == k, first, p)
            r = jnp.where(spot == k, second, r)
        applies = jnp.where((p >= 0) & keep(p, r), 1, 0)
        if swapped:
            p, r = (
                jnp.where(in_rows(x), x + 10, jnp.where(x > CORE, x - 10, x)) for x in (p, r)
            )
        if device is not None:
            held = jnp.full(shape, device, jnp.int32)
            for place in (p, r):
                bit = lax.shift_right_logical(held, jnp.maximum(place - LOCAL, 0)) & 1
                applies = applies & jnp.where(place >= LOCAL, bit, 1)
        return p, r, applies

    def row_bit(place, applies):
        return jnp.where(applies == 1, jnp.where(in_rows(place), place - 7, 8), 31)

    def column_bit(place):
        return jnp.where((place >= 0) & (place < 7), place, jnp.where(place == HALF, 7, 8))

    p, r, applies = shifts((1, 16), 1)
    row = iota((SIDE, 16), 0) ^ (FLIP if swapped else 0) | SIDE
    row = lax.shift_right_logical(row, jnp.broadcast_to(row_bit(p, applies), row.shape)) & (
        lax.shift_right_logical(row, jnp.broadcast_to(row_bit(r, applies), row.shape))
    )
    p, r, _ = shifts((16, 1), 0)
    column = iota((16, SIDE), 1) | SIDE
    column = lax.shift_right_logical(column, jnp.broadcast_to(column_bit(p), column.shape)) & (
        lax.shift_right_logical(column, jnp.broadcast_to(column_bit(r), column.shape))
    )
    count = jnp.dot(
        (row & 1).astype(jnp.float32).astype(jnp.bfloat16),
        (column & 1).astype(jnp.float32).astype(jnp.bfloat16),
        preferred_element_type=jnp.float32,
    )
    return (1 - 2 * (count.astype(jnp.int32) & 1)).astype(jnp.float32)


def in_rows(place):
    return (place >= 7) & (place < HALF)


def all_local(p, r):
    return (p < LOCAL) & (r < LOCAL)


def trade_bits(work, trades):
    lane = iota((SIDE, LANES), 1)
    row = iota((SIDE, LANES), 0)
    for bit in range(8):
        taken = trades[bit]
        step = 1 << bit

        @pl.when(taken == LANES)
        def _():
            row_up = (row & step) != 0
            first = work[:, :LANES]
            second = work[:, LANES:]
            work[:, :LANES] = jnp.where(row_up, pltpu.roll(second, step, 0), first)
            work[:, LANES:] = jnp.where(row_up, second, pltpu.roll(first, SIDE - step, 0))

        @pl.when((taken != 0) & (taken < LANES))
        def _():
            lane_up = (lane & taken) != 0
            row_up = (row & step) != 0
            for half in range(2):
                columns = slice(half * LANES, half * LANES + LANES)
                held = work[:, columns]
                from_later = pltpu.roll(pltpu.roll(held, SIDE - step, 0), taken, 1)
                from_sooner = pltpu.roll(pltpu.roll(held, step, 0), LANES - taken, 1)
                moved = jnp.where(lane_up, from_later, from_sooner)
                work[:, columns] = jnp.where(row_up == lane_up, held, moved)

def first_kernel(angles_in, pairings_in, state_in, out, plan, work, state, angles, pairings, arrived):
    copies = [
        pltpu.make_async_copy(source, target, arrived.at[slot])
        for slot, (source, target) in enumerate(
            ((angles_in, angles), (pairings_in, pairings), (state_in, state))
        )
    ]
    for copy in copies:
        copy.start()
    for copy in copies:
        copy.wait()
    of_device = jnp.int32(((1 << 25) - 1) - ((1 << LOCAL) - 1))
    apart = partners_of(pairings, 0, of_device)
    bound = apart & partners_of(pairings, 1, of_device) & ((1 << LOCAL) - 1)
    trades, stuck = choose_trades(bound)
    held = qubits_at(trades)
    plan[0] = stuck
    plan[1] = apart
    for place in range(LOCAL):
        plan[2 + place] = held[place]
    for bit in range(8):
        plan[18 + bit] = trades[bit]
    entries = [(0, q, angles[0, q]) for q in range(LOCAL)]
    for place in ROW_PLACES:
        late = lax.shift_right_logical(apart, held[place]) & 1
        entries.append((1, place, jnp.where(late == 1, 0.0, angles[1, held[place]])))
    turns = trig(angle_table(entries))
    masks = bit_masks()
    rows = kron_matrix(masks, turns, 0, ROW_PLACES, False)
    columns = kron_matrix(masks, turns, 0, LANE_PLACES + [HALF], True)
    early = kron_matrix(masks, turns, 1, ROW_PLACES, False)
    pairs = [(pairings[0, 2 * k], pairings[0, 2 * k + 1]) for k in range(PAIRS)]
    sign = sign_array(pairs, all_local)
    value = on_columns(on_rows(rows, load_matrix(state)), columns) * sign
    work[...] = value
    trade_bits(work, trades)
    store_pieces(out, on_rows(early, work[...]))


CHIP_1, CHIP_2, CHIP_3, COLUMN_2, ROW_2, ROW_3, COLUMN_3 = range(7)
MINE_1, OTHER_1, MINE_2, OTHER_2, SIGN_LATE, SIGN_3 = range(6)


def prepare_kernel(angles, pairings, plan, high, low, sign, table, places):
    stuck, apart = plan[0], plan[1]
    held = [plan[2 + place] for place in range(LOCAL)]
    waiting = partners_of(pairings, 1, stuck)
    for place in range(LOCAL):
        places[held[place]] = jnp.int32(place)
    for place in range(LOCAL, 25):
        places[place] = jnp.int32(place)
    device = lax.axis_index("wide") * lax.axis_size("narrow") + lax.axis_index("narrow")
    core = device & 1
    entries = []
    for p in range(LOCAL, 25):
        waits = (waiting >> p) & 1 == 1
        entries.append((3, p, jnp.where(waits, angles[2, p], 0.0)))
        for layer in range(3):
            angle = angles[layer, p]
            if layer == 2:
                angle = jnp.where(waits, 0.0, angle)
            if p == CORE:
                entries.append((layer, SIGNED_CORE, jnp.where(core == 1, angle, -angle)))
            else:
                entries.append((layer, p, -angle if FLIP >> (p - 17) & 1 else angle))
    for p in LANE_PLACES + [HALF]:
        entries += [(1, p, angles[1, held[p]]), (2, p, angles[2, held[p]])]
    for p in ROW_PLACES:
        late = lax.shift_right_logical(apart, held[p]) & 1
        entries.append((1, p, jnp.where(late == 1, angles[1, held[p]], 0.0)))
        entries.append((2, p, angles[2, held[p]]))
    turns = trig(angle_table(entries))
    table[0:8, :], table[8:16, :] = turns
    masks = bit_masks()
    for slot, layer, spots, transposed in (
        (CHIP_1, 0, CHIP_PLACES, False),
        (CHIP_2, 1, CHIP_PLACES, False),
        (CHIP_3, 2, CHIP_PLACES, False),
        (COLUMN_2, 1, LANE_PLACES + [HALF], True),
        (ROW_2, 1, ROW_PLACES, False),
        (ROW_3, 2, ROW_PLACES, False),
        (COLUMN_3, 2, LANE_PLACES + [HALF], True),
    ):
        high[slot], low[slot] = kron_matrix(masks, turns, layer, spots, transposed)

    def pairs_of(layer):
        return [
            (places[pairings[layer, 2 * k]], places[pairings[layer, 2 * k + 1]])
            for k in range(PAIRS)
        ]

    def is_stuck(place):
        mask = jnp.full(place.shape, stuck, jnp.int32)
        return (lax.shift_right_logical(mask, jnp.maximum(place, 0)) & 1) == 1

    def local_or_stuck(p, r):
        return all_local(p, r) | is_stuck(p) | is_stuck(r)

    def on_device(p, r):
        return (p >= LOCAL) | (r >= LOCAL)

    def on_device_not_stuck(p, r):
        return on_device(p, r) & ~(is_stuck(p) | is_stuck(r))

    chip = lax.shift_left(lax.shift_right_logical(device, 1) ^ FLIP, 1)
    mine, other = chip | core, chip | (1 - core)
    sign[MINE_1] = sign_array(pairs_of(0), on_device, mine, True)
    sign[OTHER_1] = sign_array(pairs_of(0), on_device, other, True)
    sign[MINE_2] = sign_array(pairs_of(1), on_device_not_stuck, mine, True)
    sign[OTHER_2] = sign_array(pairs_of(1), on_device_not_stuck, other, True)
    sign[SIGN_LATE] = sign_array(pairs_of(1), local_or_stuck, device)
    sign[SIGN_3] = sign_array(pairs_of(2), lambda p, r: p == p, device)


def second_kernel(mine_ref, other_ref, high, low, sign, table, out):
    def matrix(slot):
        return high[slot], low[slot]

    def core_turn(layer):
        c = table[layer : layer + 1, SIGNED_CORE : SIGNED_CORE + 1]
        s = table[8 + layer : 9 + layer, SIGNED_CORE : SIGNED_CORE + 1]
        return c, s

    mine = on_rows(matrix(CHIP_1), load_pieces(mine_ref))
    other = on_rows(matrix(CHIP_1), load_pieces(other_ref))
    c, s = core_turn(0)
    mine, other = c * mine + s * other, c * other - s * mine
    mine, other = mine * sign[MINE_1], other * sign[OTHER_1]
    c, s = core_turn(1)
    mine, other = c * mine + s * other, c * other - s * mine
    mine = on_columns(on_rows(matrix(CHIP_2), mine), matrix(COLUMN_2)) * sign[MINE_2]
    other = on_columns(on_rows(matrix(CHIP_2), other), matrix(COLUMN_2)) * sign[OTHER_2]
    c, s = core_turn(2)
    store_pieces(out, on_rows(matrix(CHIP_3), c * mine + s * other))


def third_kernel(front, back, plan, high, low, sign, table, state, out, work):
    def matrix(slot):
        return high[slot], low[slot]

    if front:
        value = on_rows(matrix(ROW_2), load_pieces(state)) * sign[SIGN_LATE]
        value = on_columns(on_rows(matrix(ROW_3), value), matrix(COLUMN_3))
    else:
        value = load_matrix(state)
    if back:
        work[...] = value * sign[SIGN_3]
        trade_bits(work, [plan[18 + bit] for bit in range(8)])
        value = work[...]
    store_matrix(out, value)


def call(kernel, in_spaces, out_shapes, scratch, flops, limit):
    specs = [pl.BlockSpec(memory_space=space) for space in in_spaces]
    outs = [jax.ShapeDtypeStruct(shape, dtype) for shape, dtype, _ in out_shapes]
    out_specs = [pl.BlockSpec(memory_space=space) for _, _, space in out_shapes]
    return pl.pallas_call(
        kernel,
        in_specs=specs,
        out_shape=outs,
        out_specs=out_specs,
        scratch_shapes=scratch,
        compiler_params=pltpu.CompilerParams(vmem_limit_bytes=limit * 1024 * 1024),
        cost_estimate=pl.CostEstimate(flops=flops, bytes_accessed=4_000_000, transcendentals=0),
    )


def shards(initial_state, angles, pairings):
    V, S = pltpu.VMEM, pltpu.SMEM
    rows = 2 * SIDE
    flat = ((rows, LANES), jnp.float32, V)
    work = [pltpu.VMEM((SIDE, SIDE), jnp.float32)]
    product_flops = 3 * 2 * SIDE**3

    devices = lax.axis_size(AXES)
    chips = [[2 * (i ^ FLIP) + core for i in range(devices // 2)] for core in range(2)]

    def across(value):
        value = value.reshape(SIDE, SIDE)
        value = lax.all_to_all(value, AXES, 0, 0, tiled=True, axis_index_groups=chips)
        return value.reshape(rows, LANES)

    def beside(value):
        return lax.ppermute(value, AXES, [(d, d ^ 1) for d in range(devices)])

    fetched = [
        pltpu.VMEM((rows, LANES), jnp.float32),
        pltpu.SMEM(angles.shape, jnp.float32),
        pltpu.SMEM(pairings.shape, jnp.int32),
        pltpu.SemaphoreType.DMA((3,)),
    ]
    state, plan = call(
        first_kernel,
        [pltpu.HBM] * 3,
        [flat, ((26,), jnp.int32, S)],
        work + fetched,
        3 * product_flops,
        60,
    )(angles, pairings, initial_state.reshape(rows, LANES))
    state = across(state)
    prepared = call(
        prepare_kernel,
        [S, S, S],
        [
            ((7, SIDE, SIDE), jnp.bfloat16, V),
            ((7, SIDE, SIDE), jnp.bfloat16, V),
            ((6, SIDE, SIDE), jnp.float32, V),
            ((16, LANES), jnp.float32, V),
        ],
        [pltpu.SMEM((25,), jnp.int32)],
        40 * product_flops,
        32,
    )(angles, pairings, plan)
    stuck = plan[0] != 0
    state, stuck, prepared = lax.optimization_barrier((state, stuck, prepared))
    (state,) = call(second_kernel, [V] * 6, [flat], [], 7 * product_flops, 32)(
        state, beside(state), *prepared
    )
    state, stuck = lax.optimization_barrier((across(state), stuck))

    def third(value, front, back):
        kernel = functools.partial(third_kernel, front, back)
        return call(kernel, [S] + [V] * 5, [flat], work, 3 * product_flops, 32)(
            plan, *prepared, value
        )[0]

    def finish(value):
        return third(value, True, True).reshape(-1)

    def finish_slowly(value):
        value = third(value, True, False)
        table = prepared[3]
        device = lax.axis_index(AXES)
        for bit in range(9):
            route = [(d, d ^ 1 << bit) for d in range(devices)]
            other = lax.ppermute(value, AXES, route)
            c, s = table[3, LOCAL + bit], table[11, LOCAL + bit]
            upper = lax.shift_right_logical(device, bit) & 1 == 1
            value = c * value + jnp.where(upper, s, -s) * other
        return third(value, False, True).reshape(-1)

    return lax.cond(stuck, finish_slowly, finish, state)


def solution(mesh):
    return jax.shard_map(
        shards,
        mesh=mesh,
        in_specs=(P(AXES), P(), P()),
        out_specs=P(AXES),
        check_vma=False,
    )
```

```python
import functools

import jax
import jax.numpy as jnp
from jax import lax
from jax.experimental import pallas as pl
from jax.experimental.pallas import tpu as pltpu
from jax.sharding import PartitionSpec as P

SIDE = 256
LANES = 128
LOCAL = 16
CORE = 16
SIGNED_CORE = 25
PAIRS = 12
FLIP = 0b10101000
CHIP_BITS = [7, 5, 3, 6, 4, 2, 1, 0]
ROW_FLIP = sum((FLIP >> bit & 1) << k for k, bit in enumerate(CHIP_BITS))
AXES = ("wide", "narrow")
LANE_PLACES = list(range(7))
ROW_PLACES = list(range(7, 15))
HALF = 15
CHIP_PLACES = [17 + bit for bit in CHIP_BITS]


def trig(angle):
    t = angle * 0.5
    u = t * t
    sine = 1.0 / 6227020800
    for term in (-1.0 / 39916800, 1.0 / 362880, -1.0 / 5040, 1.0 / 120, -1.0 / 6, 1.0):
        sine = sine * u + term
    cosine = -1.0 / 87178291200
    for term in (1.0 / 479001600, -1.0 / 3628800, 1.0 / 40320, -1.0 / 720, 1.0 / 24, -0.5, 1.0):
        cosine = cosine * u + term
    return cosine, sine * t


def iota(shape, axis):
    return lax.broadcasted_iota(jnp.int32, shape, axis)


def choose_trades(bound):
    free = (~bound & 127) | (lax.shift_right_logical(~bound, HALF) & 1) * LANES
    stuck = jnp.int32(0)
    trades = []
    for place in ROW_PLACES:
        wanted = bound & (1 << place)
        taken = jnp.where(wanted != 0, free & -free, 0)
        stuck = stuck | jnp.where(taken == 0, wanted, 0)
        free = free & ~taken
        trades.append(taken)
    return trades, stuck


def partners_of(pairings, layer, mask):
    found = jnp.int32(0)
    one = jnp.int32(1)
    for k in range(PAIRS):
        p, r = pairings[layer, 2 * k], pairings[layer, 2 * k + 1]
        found = found | lax.shift_left(lax.shift_right_logical(mask, r) & one, p)
        found = found | lax.shift_left(lax.shift_right_logical(mask, p) & one, r)
    return found


def qubits_at(trades):
    table = [jnp.int32(place) for place in range(LOCAL)]
    for lane in range(8):
        own = HALF if lane == 7 else lane
        for place in ROW_PLACES:
            table[own] = jnp.where(trades[place - 7] == 1 << lane, place, table[own])
            table[place] = jnp.where(trades[place - 7] == 1 << lane, own, table[place])
    return table


def angle_table(entries):
    spot = iota((8, LANES), 0) * LANES + iota((8, LANES), 1)
    table = jnp.zeros((8, LANES), jnp.float32)
    for row, lane, value in entries:
        table = jnp.where(spot == row * LANES + lane, value, table)
    return table


def bit_masks():
    i, j = iota((LANES, LANES), 0), iota((LANES, LANES), 1)
    same = [((i ^ j) >> b) & 1 == 0 for b in range(7)]
    upper = [(i >> b) & 1 == 1 for b in range(7)]
    return same, upper


def kron_matrix(masks, turns, row, places, transposed):
    same, upper = masks
    cosines, sines = turns

    def turn(place):
        c = cosines[row : row + 1, place : place + 1]
        s = sines[row : row + 1, place : place + 1]
        return c, -s if transposed else s

    total = None
    for b in range(7):
        c, s = turn(places[b])
        factor = jnp.where(same[b], c, jnp.where(upper[b], s, -s))
        total = factor if total is None else total * factor
    c, s = turn(places[7])
    top = jnp.concatenate([total * c, total * -s], axis=1)
    low = jnp.concatenate([total * s, total * c], axis=1)
    return parts(jnp.concatenate([top, low], axis=0))


def parts(value):
    high = value.astype(jnp.bfloat16)
    low = (value - high.astype(jnp.float32)).astype(jnp.bfloat16)
    return high, low


def product(left, right):
    (lh, ll), (rh, rl) = left, right
    a = jnp.concatenate([lh, lh, ll], axis=1)
    b = jnp.concatenate([rh, rl, rh], axis=0)
    return jnp.dot(a, b, preferred_element_type=jnp.float32)


def on_rows(matrix, value):
    return product(matrix, parts(value))


def on_columns(value, matrix):
    return product(parts(value), matrix)


def load_matrix(ref):
    return jnp.concatenate([ref[:SIDE, :], ref[SIDE:, :]], axis=1)


def store_matrix(ref, value):
    ref[:SIDE, :] = value[:, :LANES]
    ref[SIDE:, :] = value[:, LANES:]


def load_pieces(ref):
    first, second = pl.ds(0, SIDE, stride=2), pl.ds(1, SIDE, stride=2)
    return jnp.concatenate([ref[first, :], ref[second, :]], axis=1)


def store_pieces(ref, value):
    ref[pl.ds(0, SIDE, stride=2), :] = value[:, :LANES]
    ref[pl.ds(1, SIDE, stride=2), :] = value[:, LANES:]


def sign_array(pairs, keep, device=None, swapped=False):
    def shifts(shape, axis):
        spot = iota(shape, axis)
        p = jnp.full(shape, -1, jnp.int32)
        r = p
        for k, (first, second) in enumerate(pairs):
            p = jnp.where(spot == k, first, p)
            r = jnp.where(spot == k, second, r)
        applies = jnp.where((p >= 0) & keep(p, r), 1, 0)
        if swapped:
            p, r = exchanged(p), exchanged(r)
        if device is not None:
            held = jnp.full(shape, device, jnp.int32)
            for place in (p, r):
                bit = lax.shift_right_logical(held, jnp.maximum(place - LOCAL, 0)) & 1
                applies = applies & jnp.where(place >= LOCAL, bit, 1)
        return p, r, applies

    def row_bit(place, applies):
        return jnp.where(applies == 1, jnp.where(in_rows(place), place - 7, 8), 31)

    def column_bit(place):
        return jnp.where((place >= 0) & (place < 7), place, jnp.where(place == HALF, 7, 8))

    p, r, applies = shifts((1, 16), 1)
    row = iota((SIDE, 16), 0) ^ (ROW_FLIP if swapped else 0) | SIDE
    row = lax.shift_right_logical(row, jnp.broadcast_to(row_bit(p, applies), row.shape)) & (
        lax.shift_right_logical(row, jnp.broadcast_to(row_bit(r, applies), row.shape))
    )
    p, r, _ = shifts((16, 1), 0)
    column = iota((16, SIDE), 1) | SIDE
    column = lax.shift_right_logical(column, jnp.broadcast_to(column_bit(p), column.shape)) & (
        lax.shift_right_logical(column, jnp.broadcast_to(column_bit(r), column.shape))
    )
    count = jnp.dot(
        (row & 1).astype(jnp.float32).astype(jnp.bfloat16),
        (column & 1).astype(jnp.float32).astype(jnp.bfloat16),
        preferred_element_type=jnp.float32,
    )
    return (1 - 2 * (count.astype(jnp.int32) & 1)).astype(jnp.float32)


def in_rows(place):
    return (place >= 7) & (place < HALF)


def exchanged(place):
    moved = place
    for row_place, chip_place in zip(ROW_PLACES, CHIP_PLACES):
        moved = jnp.where(place == row_place, chip_place, moved)
        moved = jnp.where(place == chip_place, row_place, moved)
    return moved


def all_local(p, r):
    return (p < LOCAL) & (r < LOCAL)


def trade_bits(work, trades):
    lane = iota((SIDE, LANES), 1)
    row = iota((SIDE, LANES), 0)
    for bit in range(8):
        taken = trades[bit]
        step = 1 << bit

        @pl.when(taken == LANES)
        def _():
            row_up = (row & step) != 0
            first = work[:, :LANES]
            second = work[:, LANES:]
            work[:, :LANES] = jnp.where(row_up, pltpu.roll(second, step, 0), first)
            work[:, LANES:] = jnp.where(row_up, second, pltpu.roll(first, SIDE - step, 0))

        @pl.when((taken != 0) & (taken < LANES))
        def _():
            lane_up = (lane & taken) != 0
            row_up = (row & step) != 0
            for half in range(2):
                columns = slice(half * LANES, half * LANES + LANES)
                held = work[:, columns]
                from_later = pltpu.roll(pltpu.roll(held, SIDE - step, 0), taken, 1)
                from_sooner = pltpu.roll(pltpu.roll(held, step, 0), LANES - taken, 1)
                moved = jnp.where(lane_up, from_later, from_sooner)
                work[:, columns] = jnp.where(row_up == lane_up, held, moved)

def first_kernel(angles_in, pairings_in, state_in, out, plan, work, state, angles, pairings, arrived):
    copies = [
        pltpu.make_async_copy(source, target, arrived.at[slot])
        for slot, (source, target) in enumerate(
            ((angles_in, angles), (pairings_in, pairings), (state_in, state))
        )
    ]
    for copy in copies:
        copy.start()
    for copy in copies:
        copy.wait()
    of_device = jnp.int32(((1 << 25) - 1) - ((1 << LOCAL) - 1))
    apart = partners_of(pairings, 0, of_device)
    bound = apart & partners_of(pairings, 1, of_device) & ((1 << LOCAL) - 1)
    trades, stuck = choose_trades(bound)
    held = qubits_at(trades)
    plan[0] = stuck
    plan[1] = apart
    for place in range(LOCAL):
        plan[2 + place] = held[place]
    for bit in range(8):
        plan[18 + bit] = trades[bit]
    entries = [(0, q, angles[0, q]) for q in range(LOCAL)]
    for place in ROW_PLACES:
        late = lax.shift_right_logical(apart, held[place]) & 1
        entries.append((1, place, jnp.where(late == 1, 0.0, angles[1, held[place]])))
    turns = trig(angle_table(entries))
    masks = bit_masks()
    rows = kron_matrix(masks, turns, 0, ROW_PLACES, False)
    columns = kron_matrix(masks, turns, 0, LANE_PLACES + [HALF], True)
    early = kron_matrix(masks, turns, 1, ROW_PLACES, False)
    pairs = [(pairings[0, 2 * k], pairings[0, 2 * k + 1]) for k in range(PAIRS)]
    sign = sign_array(pairs, all_local)
    value = on_columns(on_rows(rows, load_matrix(state)), columns) * sign
    work[...] = value
    trade_bits(work, trades)
    store_pieces(out, on_rows(early, work[...]))


CHIP_1, CHIP_2, CHIP_3, COLUMN_2, ROW_2, ROW_3, COLUMN_3 = range(7)
MINE_1, OTHER_1, MINE_2, OTHER_2, SIGN_LATE, SIGN_3 = range(6)


def prepare_kernel(angles, pairings, plan, high, low, sign, table, places):
    stuck, apart = plan[0], plan[1]
    held = [plan[2 + place] for place in range(LOCAL)]
    waiting = partners_of(pairings, 1, stuck)
    for place in range(LOCAL):
        places[held[place]] = jnp.int32(place)
    for place in range(LOCAL, 25):
        places[place] = jnp.int32(place)
    device = lax.axis_index("wide") * lax.axis_size("narrow") + lax.axis_index("narrow")
    core = device & 1
    entries = []
    for p in range(LOCAL, 25):
        waits = (waiting >> p) & 1 == 1
        entries.append((3, p, jnp.where(waits, angles[2, p], 0.0)))
        for layer in range(3):
            angle = angles[layer, p]
            if layer == 2:
                angle = jnp.where(waits, 0.0, angle)
            if p == CORE:
                entries.append((layer, SIGNED_CORE, jnp.where(core == 1, angle, -angle)))
            else:
                entries.append((layer, p, -angle if FLIP >> (p - 17) & 1 else angle))
    for p in LANE_PLACES + [HALF]:
        entries += [(1, p, angles[1, held[p]]), (2, p, angles[2, held[p]])]
    for p in ROW_PLACES:
        late = lax.shift_right_logical(apart, held[p]) & 1
        entries.append((1, p, jnp.where(late == 1, angles[1, held[p]], 0.0)))
        entries.append((2, p, angles[2, held[p]]))
    turns = trig(angle_table(entries))
    table[0:8, :], table[8:16, :] = turns
    masks = bit_masks()
    for slot, layer, spots, transposed in (
        (CHIP_1, 0, CHIP_PLACES, False),
        (CHIP_2, 1, CHIP_PLACES, False),
        (CHIP_3, 2, CHIP_PLACES, False),
        (COLUMN_2, 1, LANE_PLACES + [HALF], True),
        (ROW_2, 1, ROW_PLACES, False),
        (ROW_3, 2, ROW_PLACES, False),
        (COLUMN_3, 2, LANE_PLACES + [HALF], True),
    ):
        high[slot], low[slot] = kron_matrix(masks, turns, layer, spots, transposed)

    def pairs_of(layer):
        return [
            (places[pairings[layer, 2 * k]], places[pairings[layer, 2 * k + 1]])
            for k in range(PAIRS)
        ]

    def is_stuck(place):
        mask = jnp.full(place.shape, stuck, jnp.int32)
        return (lax.shift_right_logical(mask, jnp.maximum(place, 0)) & 1) == 1

    def local_or_stuck(p, r):
        return all_local(p, r) | is_stuck(p) | is_stuck(r)

    def on_device(p, r):
        return (p >= LOCAL) | (r >= LOCAL)

    def on_device_not_stuck(p, r):
        return on_device(p, r) & ~(is_stuck(p) | is_stuck(r))

    chip = lax.shift_left(lax.shift_right_logical(device, 1) ^ FLIP, 1)
    mine, other = chip | core, chip | (1 - core)
    sign[MINE_1] = sign_array(pairs_of(0), on_device, mine, True)
    sign[OTHER_1] = sign_array(pairs_of(0), on_device, other, True)
    sign[MINE_2] = sign_array(pairs_of(1), on_device_not_stuck, mine, True)
    sign[OTHER_2] = sign_array(pairs_of(1), on_device_not_stuck, other, True)
    sign[SIGN_LATE] = sign_array(pairs_of(1), local_or_stuck, device)
    sign[SIGN_3] = sign_array(pairs_of(2), lambda p, r: p == p, device)


def second_kernel(mine_ref, other_ref, high, low, sign, table, out):
    def matrix(slot):
        return high[slot], low[slot]

    def core_turn(layer):
        c = table[layer : layer + 1, SIGNED_CORE : SIGNED_CORE + 1]
        s = table[8 + layer : 9 + layer, SIGNED_CORE : SIGNED_CORE + 1]
        return c, s

    mine = on_rows(matrix(CHIP_1), load_pieces(mine_ref))
    other = on_rows(matrix(CHIP_1), load_pieces(other_ref))
    c, s = core_turn(0)
    mine, other = c * mine + s * other, c * other - s * mine
    mine, other = mine * sign[MINE_1], other * sign[OTHER_1]
    c, s = core_turn(1)
    mine, other = c * mine + s * other, c * other - s * mine
    mine = on_columns(on_rows(matrix(CHIP_2), mine), matrix(COLUMN_2)) * sign[MINE_2]
    other = on_columns(on_rows(matrix(CHIP_2), other), matrix(COLUMN_2)) * sign[OTHER_2]
    c, s = core_turn(2)
    store_pieces(out, on_rows(matrix(CHIP_3), c * mine + s * other))


def third_kernel(front, back, plan, high, low, sign, table, state, out, work):
    def matrix(slot):
        return high[slot], low[slot]

    if front:
        value = on_rows(matrix(ROW_2), load_pieces(state)) * sign[SIGN_LATE]
        value = on_columns(on_rows(matrix(ROW_3), value), matrix(COLUMN_3))
    else:
        value = load_matrix(state)
    if back:
        work[...] = value * sign[SIGN_3]
        trade_bits(work, [plan[18 + bit] for bit in range(8)])
        value = work[...]
    store_matrix(out, value)


def call(kernel, in_spaces, out_shapes, scratch, flops, limit):
    specs = [pl.BlockSpec(memory_space=space) for space in in_spaces]
    outs = [jax.ShapeDtypeStruct(shape, dtype) for shape, dtype, _ in out_shapes]
    out_specs = [pl.BlockSpec(memory_space=space) for _, _, space in out_shapes]
    return pl.pallas_call(
        kernel,
        in_specs=specs,
        out_shape=outs,
        out_specs=out_specs,
        scratch_shapes=scratch,
        compiler_params=pltpu.CompilerParams(vmem_limit_bytes=limit * 1024 * 1024),
        cost_estimate=pl.CostEstimate(flops=flops, bytes_accessed=4_000_000, transcendentals=0),
    )


def shards(initial_state, angles, pairings):
    V, S = pltpu.VMEM, pltpu.SMEM
    rows = 2 * SIDE
    flat = ((rows, LANES), jnp.float32, V)
    work = [pltpu.VMEM((SIDE, SIDE), jnp.float32)]
    product_flops = 3 * 2 * SIDE**3

    devices = lax.axis_size(AXES)
    order = [
        sum((row >> k & 1) << bit for k, bit in enumerate(CHIP_BITS)) ^ FLIP for row in range(SIDE)
    ]
    chips = [[2 * chip + core for chip in order] for core in range(2)]

    def across(value):
        value = value.reshape(SIDE, SIDE)
        value = lax.all_to_all(value, AXES, 0, 0, tiled=True, axis_index_groups=chips)
        return value.reshape(rows, LANES)

    def beside(value):
        return lax.ppermute(value, AXES, [(d, d ^ 1) for d in range(devices)])

    fetched = [
        pltpu.VMEM((rows, LANES), jnp.float32),
        pltpu.SMEM(angles.shape, jnp.float32),
        pltpu.SMEM(pairings.shape, jnp.int32),
        pltpu.SemaphoreType.DMA((3,)),
    ]
    state, plan = call(
        first_kernel,
        [pltpu.HBM] * 3,
        [flat, ((26,), jnp.int32, S)],
        work + fetched,
        3 * product_flops,
        60,
    )(angles, pairings, initial_state.reshape(rows, LANES))
    state = across(state)
    prepared = call(
        prepare_kernel,
        [S, S, S],
        [
            ((7, SIDE, SIDE), jnp.bfloat16, V),
            ((7, SIDE, SIDE), jnp.bfloat16, V),
            ((6, SIDE, SIDE), jnp.float32, V),
            ((16, LANES), jnp.float32, V),
        ],
        [pltpu.SMEM((25,), jnp.int32)],
        40 * product_flops,
        32,
    )(angles, pairings, plan)
    stuck = plan[0] != 0
    state, stuck, prepared = lax.optimization_barrier((state, stuck, prepared))
    (state,) = call(second_kernel, [V] * 6, [flat], [], 7 * product_flops, 32)(
        state, beside(state), *prepared
    )
    state, stuck = lax.optimization_barrier((across(state), stuck))

    def third(value, front, back):
        kernel = functools.partial(third_kernel, front, back)
        return call(kernel, [S] + [V] * 5, [flat], work, 3 * product_flops, 32)(
            plan, *prepared, value
        )[0]

    def finish(value):
        return third(value, True, True).reshape(-1)

    def finish_slowly(value):
        value = third(value, True, False)
        table = prepared[3]
        device = lax.axis_index(AXES)
        for bit in range(9):
            route = [(d, d ^ 1 << bit) for d in range(devices)]
            other = lax.ppermute(value, AXES, route)
            c, s = table[3, LOCAL + bit], table[11, LOCAL + bit]
            upper = lax.shift_right_logical(device, bit) & 1 == 1
            value = c * value + jnp.where(upper, s, -s) * other
        return third(value, False, True).reshape(-1)

    return lax.cond(stuck, finish_slowly, finish, state)


def solution(mesh):
    return jax.shard_map(
        shards,
        mesh=mesh,
        in_specs=(P(AXES), P(), P()),
        out_specs=P(AXES),
        check_vma=False,
    )
```

```python
import functools

import jax
import jax.numpy as jnp
from jax import lax
from jax.experimental import pallas as pl
from jax.experimental.pallas import tpu as pltpu
from jax.sharding import PartitionSpec as P

SIDE = 256
LANES = 128
LOCAL = 16
CORE = 16
SIGNED_CORE = 25
PAIRS = 12
FLIP = 0b10101000
CHIP_BITS = [7, 5, 3, 6, 4, 2, 1, 0]
ROW_FLIP = sum((FLIP >> bit & 1) << k for k, bit in enumerate(CHIP_BITS))
AXES = ("wide", "narrow")
LANE_PLACES = list(range(7))
ROW_PLACES = list(range(7, 15))
HALF = 15
CHIP_PLACES = [17 + bit for bit in CHIP_BITS]


def trig(angle):
    t = angle * 0.5
    u = t * t
    sine = 1.0 / 6227020800
    for term in (-1.0 / 39916800, 1.0 / 362880, -1.0 / 5040, 1.0 / 120, -1.0 / 6, 1.0):
        sine = sine * u + term
    cosine = -1.0 / 87178291200
    for term in (1.0 / 479001600, -1.0 / 3628800, 1.0 / 40320, -1.0 / 720, 1.0 / 24, -0.5, 1.0):
        cosine = cosine * u + term
    return cosine, sine * t


def iota(shape, axis):
    return lax.broadcasted_iota(jnp.int32, shape, axis)


def choose_trades(bound):
    free = (~bound & 127) | (lax.shift_right_logical(~bound, HALF) & 1) * LANES
    stuck = jnp.int32(0)
    trades = []
    for place in ROW_PLACES:
        wanted = bound & (1 << place)
        taken = jnp.where(wanted != 0, free & -free, 0)
        stuck = stuck | jnp.where(taken == 0, wanted, 0)
        free = free & ~taken
        trades.append(taken)
    return trades, stuck


def partners_of(pairings, layer, mask):
    found = jnp.int32(0)
    one = jnp.int32(1)
    for k in range(PAIRS):
        p, r = pairings[layer, 2 * k], pairings[layer, 2 * k + 1]
        found = found | lax.shift_left(lax.shift_right_logical(mask, r) & one, p)
        found = found | lax.shift_left(lax.shift_right_logical(mask, p) & one, r)
    return found


def qubits_at(trades):
    table = [jnp.int32(place) for place in range(LOCAL)]
    for lane in range(8):
        own = HALF if lane == 7 else lane
        for place in ROW_PLACES:
            table[own] = jnp.where(trades[place - 7] == 1 << lane, place, table[own])
            table[place] = jnp.where(trades[place - 7] == 1 << lane, own, table[place])
    return table


def angle_table(entries):
    spot = iota((8, LANES), 0) * LANES + iota((8, LANES), 1)
    table = jnp.zeros((8, LANES), jnp.float32)
    for row, lane, value in entries:
        table = jnp.where(spot == row * LANES + lane, value, table)
    return table


def bit_masks():
    i, j = iota((LANES, LANES), 0), iota((LANES, LANES), 1)
    same = [((i ^ j) >> b) & 1 == 0 for b in range(7)]
    upper = [(i >> b) & 1 == 1 for b in range(7)]
    return same, upper


def kron_matrix(masks, turns, row, places, transposed):
    same, upper = masks
    cosines, sines = turns

    def turn(place):
        c = cosines[row : row + 1, place : place + 1]
        s = sines[row : row + 1, place : place + 1]
        return c, -s if transposed else s

    total = None
    for b in range(7):
        c, s = turn(places[b])
        factor = jnp.where(same[b], c, jnp.where(upper[b], s, -s))
        total = factor if total is None else total * factor
    c, s = turn(places[7])
    top = jnp.concatenate([total * c, total * -s], axis=1)
    low = jnp.concatenate([total * s, total * c], axis=1)
    return parts(jnp.concatenate([top, low], axis=0))


def parts(value):
    high = value.astype(jnp.bfloat16)
    low = (value - high.astype(jnp.float32)).astype(jnp.bfloat16)
    return high, low


def product(left, right):
    (lh, ll), (rh, rl) = left, right
    a = jnp.concatenate([lh, lh, ll], axis=1)
    b = jnp.concatenate([rh, rl, rh], axis=0)
    return jnp.dot(a, b, preferred_element_type=jnp.float32)


def on_rows(matrix, value):
    return product(matrix, parts(value))


def on_columns(value, matrix):
    return product(parts(value), matrix)


def load_matrix(ref):
    return jnp.concatenate([ref[:SIDE, :], ref[SIDE:, :]], axis=1)


def store_matrix(ref, value):
    ref[:SIDE, :] = value[:, :LANES]
    ref[SIDE:, :] = value[:, LANES:]


def load_pieces(ref):
    first, second = pl.ds(0, SIDE, stride=2), pl.ds(1, SIDE, stride=2)
    return jnp.concatenate([ref[first, :], ref[second, :]], axis=1)


def store_pieces(ref, value):
    ref[pl.ds(0, SIDE, stride=2), :] = value[:, :LANES]
    ref[pl.ds(1, SIDE, stride=2), :] = value[:, LANES:]


def sign_array(pairs, keep, device=None, swapped=False):
    def shifts(shape, axis):
        spot = iota(shape, axis)
        p = jnp.full(shape, -1, jnp.int32)
        r = p
        for k, (first, second) in enumerate(pairs):
            p = jnp.where(spot == k, first, p)
            r = jnp.where(spot == k, second, r)
        applies = jnp.where((p >= 0) & keep(p, r), 1, 0)
        if swapped:
            p, r = exchanged(p), exchanged(r)
        if device is not None:
            held = jnp.full(shape, device, jnp.int32)
            for place in (p, r):
                bit = lax.shift_right_logical(held, jnp.maximum(place - LOCAL, 0)) & 1
                applies = applies & jnp.where(place >= LOCAL, bit, 1)
        return p, r, applies

    def row_bit(place, applies):
        return jnp.where(applies == 1, jnp.where(in_rows(place), place - 7, 8), 31)

    def column_bit(place):
        return jnp.where((place >= 0) & (place < 7), place, jnp.where(place == HALF, 7, 8))

    p, r, applies = shifts((1, 16), 1)
    row = iota((SIDE, 16), 0) ^ (ROW_FLIP if swapped else 0) | SIDE
    row = lax.shift_right_logical(row, jnp.broadcast_to(row_bit(p, applies), row.shape)) & (
        lax.shift_right_logical(row, jnp.broadcast_to(row_bit(r, applies), row.shape))
    )
    p, r, _ = shifts((16, 1), 0)
    column = iota((16, SIDE), 1) | SIDE
    column = lax.shift_right_logical(column, jnp.broadcast_to(column_bit(p), column.shape)) & (
        lax.shift_right_logical(column, jnp.broadcast_to(column_bit(r), column.shape))
    )
    count = jnp.dot(
        (row & 1).astype(jnp.float32).astype(jnp.bfloat16),
        (column & 1).astype(jnp.float32).astype(jnp.bfloat16),
        preferred_element_type=jnp.float32,
    )
    return (1 - 2 * (count.astype(jnp.int32) & 1)).astype(jnp.float32)


def in_rows(place):
    return (place >= 7) & (place < HALF)


def exchanged(place):
    moved = place
    for row_place, chip_place in zip(ROW_PLACES, CHIP_PLACES):
        moved = jnp.where(place == row_place, chip_place, moved)
        moved = jnp.where(place == chip_place, row_place, moved)
    return moved


def all_local(p, r):
    return (p < LOCAL) & (r < LOCAL)


def trade_bits(work, trades):
    lane = iota((SIDE, LANES), 1)
    row = iota((SIDE, LANES), 0)
    for bit in range(8):
        taken = trades[bit]
        step = 1 << bit

        @pl.when(taken == LANES)
        def _():
            row_up = (row & step) != 0
            first = work[:, :LANES]
            second = work[:, LANES:]
            work[:, :LANES] = jnp.where(row_up, pltpu.roll(second, step, 0), first)
            work[:, LANES:] = jnp.where(row_up, second, pltpu.roll(first, SIDE - step, 0))

        @pl.when((taken != 0) & (taken < LANES))
        def _():
            if step >= 8:
                view = work[...].reshape(SIDE // (2 * step), 2, step, SIDE)
                for half in range(2):
                    columns = slice(half * LANES, half * LANES + LANES)
                    lower = view[:, 0, :, columns].reshape(LANES, LANES)
                    upper = view[:, 1, :, columns].reshape(LANES, LANES)
                    lane_up = (iota((LANES, LANES), 1) & taken) != 0
                    pair = [
                        jnp.where(lane_up, pltpu.roll(upper, taken, 1), lower),
                        jnp.where(lane_up, upper, pltpu.roll(lower, LANES - taken, 1)),
                    ]
                    shape = (SIDE // (2 * step), 1, step, LANES)
                    pair = jnp.concatenate([x.reshape(shape) for x in pair], axis=1)
                    work[:, columns] = pair.reshape(SIDE, LANES)
                return
            lane_up = (lane & taken) != 0
            row_up = (row & step) != 0
            for half in range(2):
                columns = slice(half * LANES, half * LANES + LANES)
                held = work[:, columns]
                from_later = pltpu.roll(pltpu.roll(held, SIDE - step, 0), taken, 1)
                from_sooner = pltpu.roll(pltpu.roll(held, step, 0), LANES - taken, 1)
                moved = jnp.where(lane_up, from_later, from_sooner)
                work[:, columns] = jnp.where(row_up == lane_up, held, moved)

def first_kernel(angles_in, pairings_in, state_in, out, plan, work, state, angles, pairings, arrived):
    copies = [
        pltpu.make_async_copy(source, target, arrived.at[slot])
        for slot, (source, target) in enumerate(
            ((angles_in, angles), (pairings_in, pairings), (state_in, state))
        )
    ]
    for copy in copies:
        copy.start()
    for copy in copies:
        copy.wait()
    of_device = jnp.int32(((1 << 25) - 1) - ((1 << LOCAL) - 1))
    apart = partners_of(pairings, 0, of_device)
    bound = apart & partners_of(pairings, 1, of_device) & ((1 << LOCAL) - 1)
    trades, stuck = choose_trades(bound)
    held = qubits_at(trades)
    plan[0] = stuck
    plan[1] = apart
    for place in range(LOCAL):
        plan[2 + place] = held[place]
    for bit in range(8):
        plan[18 + bit] = trades[bit]
    entries = [(0, q, angles[0, q]) for q in range(LOCAL)]
    for place in ROW_PLACES:
        late = lax.shift_right_logical(apart, held[place]) & 1
        entries.append((1, place, jnp.where(late == 1, 0.0, angles[1, held[place]])))
    turns = trig(angle_table(entries))
    masks = bit_masks()
    rows = kron_matrix(masks, turns, 0, ROW_PLACES, False)
    columns = kron_matrix(masks, turns, 0, LANE_PLACES + [HALF], True)
    early = kron_matrix(masks, turns, 1, ROW_PLACES, False)
    pairs = [(pairings[0, 2 * k], pairings[0, 2 * k + 1]) for k in range(PAIRS)]
    sign = sign_array(pairs, all_local)
    value = on_columns(on_rows(rows, load_matrix(state)), columns) * sign
    work[...] = value
    trade_bits(work, trades)
    store_pieces(out, on_rows(early, work[...]))


CHIP_1, CHIP_2, CHIP_3, COLUMN_2 = range(4)
ROW_2, ROW_3, COLUMN_3 = range(3)
MINE_1, OTHER_1, MINE_2, OTHER_2 = range(4)
SIGN_LATE, SIGN_3 = range(2)


def prepare_kernel(
    angles, pairings, plan, high, low, sign, last_high, last_low, last_sign, table, places
):
    stuck, apart = plan[0], plan[1]
    held = [plan[2 + place] for place in range(LOCAL)]
    waiting = partners_of(pairings, 1, stuck)
    for place in range(LOCAL):
        places[held[place]] = jnp.int32(place)
    for place in range(LOCAL, 25):
        places[place] = jnp.int32(place)
    device = lax.axis_index("wide") * lax.axis_size("narrow") + lax.axis_index("narrow")
    core = device & 1
    entries = []
    for p in range(LOCAL, 25):
        waits = (waiting >> p) & 1 == 1
        entries.append((3, p, jnp.where(waits, angles[2, p], 0.0)))
        for layer in range(3):
            angle = angles[layer, p]
            if layer == 2:
                angle = jnp.where(waits, 0.0, angle)
            if p == CORE:
                entries.append((layer, SIGNED_CORE, jnp.where(core == 1, angle, -angle)))
            else:
                entries.append((layer, p, -angle if FLIP >> (p - 17) & 1 else angle))
    for p in LANE_PLACES + [HALF]:
        entries += [(1, p, angles[1, held[p]]), (2, p, angles[2, held[p]])]
    for p in ROW_PLACES:
        late = lax.shift_right_logical(apart, held[p]) & 1
        entries.append((1, p, jnp.where(late == 1, angles[1, held[p]], 0.0)))
        entries.append((2, p, angles[2, held[p]]))
    turns = trig(angle_table(entries))
    table[0:8, :], table[8:16, :] = turns
    masks = bit_masks()
    second, third = (high, low), (last_high, last_low)
    for (to_high, to_low), slot, layer, spots, transposed in (
        (second, CHIP_1, 0, CHIP_PLACES, False),
        (second, CHIP_2, 1, CHIP_PLACES, False),
        (second, CHIP_3, 2, CHIP_PLACES, False),
        (second, COLUMN_2, 1, LANE_PLACES + [HALF], True),
        (third, ROW_2, 1, ROW_PLACES, False),
        (third, ROW_3, 2, ROW_PLACES, False),
        (third, COLUMN_3, 2, LANE_PLACES + [HALF], True),
    ):
        to_high[slot], to_low[slot] = kron_matrix(masks, turns, layer, spots, transposed)

    def pairs_of(layer):
        return [
            (places[pairings[layer, 2 * k]], places[pairings[layer, 2 * k + 1]])
            for k in range(PAIRS)
        ]

    def is_stuck(place):
        mask = jnp.full(place.shape, stuck, jnp.int32)
        return (lax.shift_right_logical(mask, jnp.maximum(place, 0)) & 1) == 1

    def local_or_stuck(p, r):
        return all_local(p, r) | is_stuck(p) | is_stuck(r)

    def on_device(p, r):
        return (p >= LOCAL) | (r >= LOCAL)

    def on_device_not_stuck(p, r):
        return on_device(p, r) & ~(is_stuck(p) | is_stuck(r))

    chip = lax.shift_left(lax.shift_right_logical(device, 1) ^ FLIP, 1)
    mine, other = chip | core, chip | (1 - core)
    sign[MINE_1] = sign_array(pairs_of(0), on_device, mine, True)
    sign[OTHER_1] = sign_array(pairs_of(0), on_device, other, True)
    sign[MINE_2] = sign_array(pairs_of(1), on_device_not_stuck, mine, True)
    sign[OTHER_2] = sign_array(pairs_of(1), on_device_not_stuck, other, True)
    last_sign[SIGN_LATE] = sign_array(pairs_of(1), local_or_stuck, device)
    last_sign[SIGN_3] = sign_array(pairs_of(2), lambda p, r: p == p, device)


def begin_kernel(state, high, low, out):
    out[...] = on_rows((high[CHIP_1], low[CHIP_1]), load_pieces(state))


def second_kernel(mine_ref, other_ref, high, low, sign, table, out):
    def matrix(slot):
        return high[slot], low[slot]

    def core_turn(layer):
        c = table[layer : layer + 1, SIGNED_CORE : SIGNED_CORE + 1]
        s = table[8 + layer : 9 + layer, SIGNED_CORE : SIGNED_CORE + 1]
        return c, s

    mine = mine_ref[...]
    other = on_rows(matrix(CHIP_1), load_pieces(other_ref))
    c, s = core_turn(0)
    mine, other = c * mine + s * other, c * other - s * mine
    mine, other = mine * sign[MINE_1], other * sign[OTHER_1]
    c, s = core_turn(1)
    mine, other = c * mine + s * other, c * other - s * mine
    both = jnp.concatenate([on_rows(matrix(CHIP_2), mine), on_rows(matrix(CHIP_2), other)], axis=0)
    both = on_columns(both, matrix(COLUMN_2))
    mine, other = both[:SIDE] * sign[MINE_2], both[SIDE:] * sign[OTHER_2]
    c, s = core_turn(2)
    store_pieces(out, on_rows(matrix(CHIP_3), c * mine + s * other))


def third_kernel(front, back, plan, high, low, sign, state, out, work):
    def matrix(slot):
        return high[slot], low[slot]

    if front:
        value = on_rows(matrix(ROW_2), load_pieces(state)) * sign[SIGN_LATE]
        value = on_columns(on_rows(matrix(ROW_3), value), matrix(COLUMN_3))
    else:
        value = load_matrix(state)
    if back:
        work[...] = value * sign[SIGN_3]
        trade_bits(work, [plan[18 + bit] for bit in range(8)])
        value = work[...]
    store_matrix(out, value)


def call(kernel, in_spaces, out_shapes, scratch, flops, limit):
    specs = [pl.BlockSpec(memory_space=space) for space in in_spaces]
    outs = [jax.ShapeDtypeStruct(shape, dtype) for shape, dtype, _ in out_shapes]
    out_specs = [pl.BlockSpec(memory_space=space) for _, _, space in out_shapes]
    return pl.pallas_call(
        kernel,
        in_specs=specs,
        out_shape=outs,
        out_specs=out_specs,
        scratch_shapes=scratch,
        compiler_params=pltpu.CompilerParams(vmem_limit_bytes=limit * 1024 * 1024),
        cost_estimate=pl.CostEstimate(flops=flops, bytes_accessed=4_000_000, transcendentals=0),
    )


def shards(initial_state, angles, pairings):
    V, S = pltpu.VMEM, pltpu.SMEM
    rows = 2 * SIDE
    flat = ((rows, LANES), jnp.float32, V)
    work = [pltpu.VMEM((SIDE, SIDE), jnp.float32)]
    product_flops = 3 * 2 * SIDE**3

    devices = lax.axis_size(AXES)
    order = [
        sum((row >> k & 1) << bit for k, bit in enumerate(CHIP_BITS)) ^ FLIP for row in range(SIDE)
    ]
    chips = [[2 * chip + core for chip in order] for core in range(2)]

    def across(value):
        value = value.reshape(SIDE, SIDE)
        value = lax.all_to_all(value, AXES, 0, 0, tiled=True, axis_index_groups=chips)
        return value.reshape(rows, LANES)

    def beside(value):
        return lax.ppermute(value, AXES, [(d, d ^ 1) for d in range(devices)])

    fetched = [
        pltpu.VMEM((rows, LANES), jnp.float32),
        pltpu.SMEM(angles.shape, jnp.float32),
        pltpu.SMEM(pairings.shape, jnp.int32),
        pltpu.SemaphoreType.DMA((3,)),
    ]
    state, plan = call(
        first_kernel,
        [pltpu.HBM] * 3,
        [flat, ((26,), jnp.int32, S)],
        work + fetched,
        3 * product_flops,
        60,
    )(angles, pairings, initial_state.reshape(rows, LANES))
    state = across(state)
    prepared = call(
        prepare_kernel,
        [S, S, S],
        [
            ((4, SIDE, SIDE), jnp.bfloat16, V),
            ((4, SIDE, SIDE), jnp.bfloat16, V),
            ((4, SIDE, SIDE), jnp.float32, V),
            ((3, SIDE, SIDE), jnp.bfloat16, V),
            ((3, SIDE, SIDE), jnp.bfloat16, V),
            ((2, SIDE, SIDE), jnp.float32, V),
            ((16, LANES), jnp.float32, V),
        ],
        [pltpu.SMEM((25,), jnp.int32)],
        40 * product_flops,
        16,
    )(angles, pairings, plan)
    stuck = plan[0] != 0
    state, stuck, prepared = lax.optimization_barrier((state, stuck, prepared))
    square = ((SIDE, SIDE), jnp.float32, V)
    (begun,) = call(begin_kernel, [V] * 3, [square], [], product_flops, 16)(state, *prepared[:2])
    table = prepared[6]
    (state,) = call(second_kernel, [V] * 6, [flat], [], 7 * product_flops, 16)(
        begun, beside(state), *prepared[:3], table
    )
    state, stuck = lax.optimization_barrier((across(state), stuck))

    def third(value, front, back):
        kernel = functools.partial(third_kernel, front, back)
        return call(kernel, [S] + [V] * 4, [flat], work, 3 * product_flops, 16)(
            plan, *prepared[3:6], value
        )[0]

    def finish(value):
        return third(value, True, True).reshape(-1)

    def finish_slowly(value):
        value = third(value, True, False)
        device = lax.axis_index(AXES)
        for bit in range(9):
            route = [(d, d ^ 1 << bit) for d in range(devices)]
            other = lax.ppermute(value, AXES, route)
            c, s = table[3, LOCAL + bit], table[11, LOCAL + bit]
            upper = lax.shift_right_logical(device, bit) & 1 == 1
            value = c * value + jnp.where(upper, s, -s) * other
        return third(value, False, True).reshape(-1)

    return lax.cond(stuck, finish_slowly, finish, state)


def solution(mesh):
    return jax.shard_map(
        shards,
        mesh=mesh,
        in_specs=(P(AXES), P(), P()),
        out_specs=P(AXES),
        check_vma=False,
    )
```

```python
import functools

import jax
import jax.numpy as jnp
from jax import lax
from jax.experimental import pallas as pl
from jax.experimental.pallas import tpu as pltpu
from jax.sharding import PartitionSpec as P

SIDE = 256
LANES = 128
LOCAL = 16
CORE = 16
SIGNED_CORE = 25
PAIRS = 12
FLIP = 0b10101000
CHIP_BITS = [7, 5, 3, 6, 4, 2, 1, 0]
ROW_FLIP = sum((FLIP >> bit & 1) << k for k, bit in enumerate(CHIP_BITS))
AXES = ("wide", "narrow")
LANE_PLACES = list(range(7))
ROW_PLACES = list(range(7, 15))
HALF = 15
CHIP_PLACES = [17 + bit for bit in CHIP_BITS]


def trig(angle):
    t = angle * 0.5
    u = t * t
    sine = 1.0 / 6227020800
    for term in (-1.0 / 39916800, 1.0 / 362880, -1.0 / 5040, 1.0 / 120, -1.0 / 6, 1.0):
        sine = sine * u + term
    cosine = -1.0 / 87178291200
    for term in (1.0 / 479001600, -1.0 / 3628800, 1.0 / 40320, -1.0 / 720, 1.0 / 24, -0.5, 1.0):
        cosine = cosine * u + term
    return cosine, sine * t


def iota(shape, axis):
    return lax.broadcasted_iota(jnp.int32, shape, axis)


def choose_trades(bound):
    free = (~bound & 127) | (lax.shift_right_logical(~bound, HALF) & 1) * LANES
    stuck = jnp.int32(0)
    trades = []
    for place in ROW_PLACES:
        wanted = bound & (1 << place)
        taken = jnp.where(wanted != 0, free & -free, 0)
        stuck = stuck | jnp.where(taken == 0, wanted, 0)
        free = free & ~taken
        trades.append(taken)
    return trades, stuck


def partners_of(pairings, layer, mask):
    found = jnp.int32(0)
    one = jnp.int32(1)
    for k in range(PAIRS):
        p, r = pairings[layer, 2 * k], pairings[layer, 2 * k + 1]
        found = found | lax.shift_left(lax.shift_right_logical(mask, r) & one, p)
        found = found | lax.shift_left(lax.shift_right_logical(mask, p) & one, r)
    return found


def qubits_at(trades):
    table = [jnp.int32(place) for place in range(LOCAL)]
    for lane in range(8):
        own = HALF if lane == 7 else lane
        for place in ROW_PLACES:
            table[own] = jnp.where(trades[place - 7] == 1 << lane, place, table[own])
            table[place] = jnp.where(trades[place - 7] == 1 << lane, own, table[place])
    return table


def angle_table(entries):
    spot = iota((8, LANES), 0) * LANES + iota((8, LANES), 1)
    table = jnp.zeros((8, LANES), jnp.float32)
    for row, lane, value in entries:
        table = jnp.where(spot == row * LANES + lane, value, table)
    return table


def bit_masks():
    i, j = iota((LANES, LANES), 0), iota((LANES, LANES), 1)
    same = [((i ^ j) >> b) & 1 == 0 for b in range(7)]
    upper = [(i >> b) & 1 == 1 for b in range(7)]
    return same, upper


def kron_matrix(masks, turns, row, places, transposed):
    same, upper = masks
    cosines, sines = turns

    def turn(place):
        c = cosines[row : row + 1, place : place + 1]
        s = sines[row : row + 1, place : place + 1]
        return c, -s if transposed else s

    total = None
    for b in range(7):
        c, s = turn(places[b])
        factor = jnp.where(same[b], c, jnp.where(upper[b], s, -s))
        total = factor if total is None else total * factor
    c, s = turn(places[7])
    top = jnp.concatenate([total * c, total * -s], axis=1)
    low = jnp.concatenate([total * s, total * c], axis=1)
    return parts(jnp.concatenate([top, low], axis=0))


def parts(value):
    high = value.astype(jnp.bfloat16)
    low = (value - high.astype(jnp.float32)).astype(jnp.bfloat16)
    return high, low


def product(left, right):
    (lh, ll), (rh, rl) = left, right
    a = jnp.concatenate([lh, lh, ll], axis=1)
    b = jnp.concatenate([rh, rl, rh], axis=0)
    return jnp.dot(a, b, preferred_element_type=jnp.float32)


def on_rows(matrix, value):
    return product(matrix, parts(value))


def on_columns(value, matrix):
    return product(parts(value), matrix)


def load_matrix(ref):
    return jnp.concatenate([ref[:SIDE, :], ref[SIDE:, :]], axis=1)


def store_matrix(ref, value):
    ref[:SIDE, :] = value[:, :LANES]
    ref[SIDE:, :] = value[:, LANES:]


def load_pieces(ref):
    first, second = pl.ds(0, SIDE, stride=2), pl.ds(1, SIDE, stride=2)
    return jnp.concatenate([ref[first, :], ref[second, :]], axis=1)


def store_pieces(ref, value):
    ref[pl.ds(0, SIDE, stride=2), :] = value[:, :LANES]
    ref[pl.ds(1, SIDE, stride=2), :] = value[:, LANES:]


def sign_array(pairs, keep, device=None, swapped=False):
    def shifts(shape, axis):
        spot = iota(shape, axis)
        p = jnp.full(shape, -1, jnp.int32)
        r = p
        for k, (first, second) in enumerate(pairs):
            p = jnp.where(spot == k, first, p)
            r = jnp.where(spot == k, second, r)
        applies = jnp.where((p >= 0) & keep(p, r), 1, 0)
        if swapped:
            p, r = exchanged(p), exchanged(r)
        if device is not None:
            held = jnp.full(shape, device, jnp.int32)
            for place in (p, r):
                bit = lax.shift_right_logical(held, jnp.maximum(place - LOCAL, 0)) & 1
                applies = applies & jnp.where(place >= LOCAL, bit, 1)
        return p, r, applies

    def row_bit(place, applies):
        return jnp.where(applies == 1, jnp.where(in_rows(place), place - 7, 8), 31)

    def column_bit(place):
        return jnp.where((place >= 0) & (place < 7), place, jnp.where(place == HALF, 7, 8))

    p, r, applies = shifts((1, 16), 1)
    row = iota((SIDE, 16), 0) ^ (ROW_FLIP if swapped else 0) | SIDE
    row = lax.shift_right_logical(row, jnp.broadcast_to(row_bit(p, applies), row.shape)) & (
        lax.shift_right_logical(row, jnp.broadcast_to(row_bit(r, applies), row.shape))
    )
    p, r, _ = shifts((16, 1), 0)
    column = iota((16, SIDE), 1) | SIDE
    column = lax.shift_right_logical(column, jnp.broadcast_to(column_bit(p), column.shape)) & (
        lax.shift_right_logical(column, jnp.broadcast_to(column_bit(r), column.shape))
    )
    count = jnp.dot(
        (row & 1).astype(jnp.float32).astype(jnp.bfloat16),
        (column & 1).astype(jnp.float32).astype(jnp.bfloat16),
        preferred_element_type=jnp.float32,
    )
    return (1 - 2 * (count.astype(jnp.int32) & 1)).astype(jnp.float32)


def in_rows(place):
    return (place >= 7) & (place < HALF)


def exchanged(place):
    moved = place
    for row_place, chip_place in zip(ROW_PLACES, CHIP_PLACES):
        moved = jnp.where(place == row_place, chip_place, moved)
        moved = jnp.where(place == chip_place, row_place, moved)
    return moved


def all_local(p, r):
    return (p < LOCAL) & (r < LOCAL)


def trade_bits(work, trades):
    lane = iota((SIDE, LANES), 1)
    row = iota((SIDE, LANES), 0)
    for bit in range(8):
        taken = trades[bit]
        step = 1 << bit

        @pl.when(taken == LANES)
        def _():
            row_up = (row & step) != 0
            first = work[:, :LANES]
            second = work[:, LANES:]
            work[:, :LANES] = jnp.where(row_up, pltpu.roll(second, step, 0), first)
            work[:, LANES:] = jnp.where(row_up, second, pltpu.roll(first, SIDE - step, 0))

        @pl.when((taken != 0) & (taken < LANES))
        def _():
            if step >= 8:
                view = work[...].reshape(SIDE // (2 * step), 2, step, SIDE)
                for half in range(2):
                    columns = slice(half * LANES, half * LANES + LANES)
                    lower = view[:, 0, :, columns].reshape(LANES, LANES)
                    upper = view[:, 1, :, columns].reshape(LANES, LANES)
                    lane_up = (iota((LANES, LANES), 1) & taken) != 0
                    pair = [
                        jnp.where(lane_up, pltpu.roll(upper, taken, 1), lower),
                        jnp.where(lane_up, upper, pltpu.roll(lower, LANES - taken, 1)),
                    ]
                    shape = (SIDE // (2 * step), 1, step, LANES)
                    pair = jnp.concatenate([x.reshape(shape) for x in pair], axis=1)
                    work[:, columns] = pair.reshape(SIDE, LANES)
                return
            lane_up = (lane & taken) != 0
            row_up = (row & step) != 0
            for half in range(2):
                columns = slice(half * LANES, half * LANES + LANES)
                held = work[:, columns]
                from_later = pltpu.roll(pltpu.roll(held, SIDE - step, 0), taken, 1)
                from_sooner = pltpu.roll(pltpu.roll(held, step, 0), LANES - taken, 1)
                moved = jnp.where(lane_up, from_later, from_sooner)
                work[:, columns] = jnp.where(row_up == lane_up, held, moved)

def first_kernel(angles_in, pairings_in, state_in, out, plan, work, state, angles, pairings, arrived):
    copies = [
        pltpu.make_async_copy(source, target, arrived.at[slot])
        for slot, (source, target) in enumerate(
            ((angles_in, angles), (pairings_in, pairings), (state_in, state))
        )
    ]
    for copy in copies:
        copy.start()
    for copy in copies:
        copy.wait()
    of_device = jnp.int32(((1 << 25) - 1) - ((1 << LOCAL) - 1))
    apart = partners_of(pairings, 0, of_device)
    bound = apart & partners_of(pairings, 1, of_device) & ((1 << LOCAL) - 1)
    trades, stuck = choose_trades(bound)
    held = qubits_at(trades)
    plan[0] = stuck
    plan[1] = apart
    for place in range(LOCAL):
        plan[2 + place] = held[place]
    for bit in range(8):
        plan[18 + bit] = trades[bit]
    entries = [(0, q, angles[0, q]) for q in range(LOCAL)]
    for place in ROW_PLACES:
        late = lax.shift_right_logical(apart, held[place]) & 1
        entries.append((1, place, jnp.where(late == 1, 0.0, angles[1, held[place]])))
    turns = trig(angle_table(entries))
    masks = bit_masks()
    rows = kron_matrix(masks, turns, 0, ROW_PLACES, False)
    columns = kron_matrix(masks, turns, 0, LANE_PLACES + [HALF], True)
    early = kron_matrix(masks, turns, 1, ROW_PLACES, False)
    pairs = [(pairings[0, 2 * k], pairings[0, 2 * k + 1]) for k in range(PAIRS)]
    sign = sign_array(pairs, all_local)
    value = on_columns(on_rows(rows, load_matrix(state)), columns) * sign
    work[...] = value
    trade_bits(work, trades)
    store_pieces(out, on_rows(early, work[...]))


CHIP_1, CHIP_2, CHIP_3, COLUMN_2 = range(4)
ROW_2, ROW_3, COLUMN_3 = range(3)
MINE_1, OTHER_1, MINE_2, OTHER_2 = range(4)
SIGN_LATE, SIGN_3 = range(2)


def prepare_kernel(
    angles, pairings, plan, high, low, sign, last_high, last_low, last_sign, table, places
):
    stuck, apart = plan[0], plan[1]
    held = [plan[2 + place] for place in range(LOCAL)]
    waiting = partners_of(pairings, 1, stuck)
    for place in range(LOCAL):
        places[held[place]] = jnp.int32(place)
    for place in range(LOCAL, 25):
        places[place] = jnp.int32(place)
    device = lax.axis_index("wide") * lax.axis_size("narrow") + lax.axis_index("narrow")
    core = device & 1
    entries = []
    for p in range(LOCAL, 25):
        waits = (waiting >> p) & 1 == 1
        entries.append((3, p, jnp.where(waits, angles[2, p], 0.0)))
        for layer in range(3):
            angle = angles[layer, p]
            if layer == 2:
                angle = jnp.where(waits, 0.0, angle)
            if p == CORE:
                entries.append((layer, SIGNED_CORE, jnp.where(core == 1, angle, -angle)))
            else:
                entries.append((layer, p, -angle if FLIP >> (p - 17) & 1 else angle))
    for p in LANE_PLACES + [HALF]:
        entries += [(1, p, angles[1, held[p]]), (2, p, angles[2, held[p]])]
    for p in ROW_PLACES:
        late = lax.shift_right_logical(apart, held[p]) & 1
        entries.append((1, p, jnp.where(late == 1, angles[1, held[p]], 0.0)))
        entries.append((2, p, angles[2, held[p]]))
    turns = trig(angle_table(entries))
    table[0:8, :], table[8:16, :] = turns
    masks = bit_masks()
    second, third = (high, low), (last_high, last_low)
    for (to_high, to_low), slot, layer, spots, transposed in (
        (second, CHIP_1, 0, CHIP_PLACES, False),
        (second, CHIP_2, 1, CHIP_PLACES, False),
        (second, CHIP_3, 2, CHIP_PLACES, False),
        (second, COLUMN_2, 1, LANE_PLACES + [HALF], True),
        (third, ROW_2, 1, ROW_PLACES, False),
        (third, ROW_3, 2, ROW_PLACES, False),
        (third, COLUMN_3, 2, LANE_PLACES + [HALF], True),
    ):
        to_high[slot], to_low[slot] = kron_matrix(masks, turns, layer, spots, transposed)

    def pairs_of(layer):
        return [
            (places[pairings[layer, 2 * k]], places[pairings[layer, 2 * k + 1]])
            for k in range(PAIRS)
        ]

    def is_stuck(place):
        mask = jnp.full(place.shape, stuck, jnp.int32)
        return (lax.shift_right_logical(mask, jnp.maximum(place, 0)) & 1) == 1

    def local_or_stuck(p, r):
        return all_local(p, r) | is_stuck(p) | is_stuck(r)

    def on_device(p, r):
        return (p >= LOCAL) | (r >= LOCAL)

    def on_device_not_stuck(p, r):
        return on_device(p, r) & ~(is_stuck(p) | is_stuck(r))

    chip = lax.shift_left(lax.shift_right_logical(device, 1) ^ FLIP, 1)
    mine, other = chip | core, chip | (1 - core)
    sign[MINE_1] = sign_array(pairs_of(0), on_device, mine, True)
    sign[OTHER_1] = sign_array(pairs_of(0), on_device, other, True)
    sign[MINE_2] = sign_array(pairs_of(1), on_device_not_stuck, mine, True)
    sign[OTHER_2] = sign_array(pairs_of(1), on_device_not_stuck, other, True)
    last_sign[SIGN_LATE] = sign_array(pairs_of(1), local_or_stuck, device)
    last_sign[SIGN_3] = sign_array(pairs_of(2), lambda p, r: p == p, device)


def begin_kernel(state, high, low, out):
    out[...] = on_rows((high[CHIP_1], low[CHIP_1]), load_pieces(state))


def second_kernel(mine_ref, other_ref, high, low, sign, table, out):
    def matrix(slot):
        return high[slot], low[slot]

    def core_turn(layer):
        c = table[layer : layer + 1, SIGNED_CORE : SIGNED_CORE + 1]
        s = table[8 + layer : 9 + layer, SIGNED_CORE : SIGNED_CORE + 1]
        return c, s

    mine = mine_ref[...]
    other = on_rows(matrix(CHIP_1), load_pieces(other_ref))
    c, s = core_turn(0)
    mine, other = c * mine + s * other, c * other - s * mine
    mine, other = mine * sign[MINE_1], other * sign[OTHER_1]
    c, s = core_turn(1)
    mine, other = c * mine + s * other, c * other - s * mine
    both = on_rows(matrix(CHIP_2), jnp.concatenate([mine, other], axis=1))
    both = jnp.concatenate([both[:, :SIDE], both[:, SIDE:]], axis=0)
    both = on_columns(both, matrix(COLUMN_2))
    mine, other = both[:SIDE] * sign[MINE_2], both[SIDE:] * sign[OTHER_2]
    c, s = core_turn(2)
    store_pieces(out, on_rows(matrix(CHIP_3), c * mine + s * other))


def third_kernel(front, back, plan, high, low, sign, state, out, work):
    def matrix(slot):
        return high[slot], low[slot]

    if front:
        value = on_rows(matrix(ROW_2), load_pieces(state)) * sign[SIGN_LATE]
        value = on_columns(on_rows(matrix(ROW_3), value), matrix(COLUMN_3))
    else:
        value = load_matrix(state)
    if back:
        work[...] = value * sign[SIGN_3]
        trade_bits(work, [plan[18 + bit] for bit in range(8)])
        value = work[...]
    store_matrix(out, value)


def call(kernel, in_spaces, out_shapes, scratch, flops, limit):
    specs = [pl.BlockSpec(memory_space=space) for space in in_spaces]
    outs = [jax.ShapeDtypeStruct(shape, dtype) for shape, dtype, _ in out_shapes]
    out_specs = [pl.BlockSpec(memory_space=space) for _, _, space in out_shapes]
    return pl.pallas_call(
        kernel,
        in_specs=specs,
        out_shape=outs,
        out_specs=out_specs,
        scratch_shapes=scratch,
        compiler_params=pltpu.CompilerParams(vmem_limit_bytes=limit * 1024 * 1024),
        cost_estimate=pl.CostEstimate(flops=flops, bytes_accessed=4_000_000, transcendentals=0),
    )


def shards(initial_state, angles, pairings):
    V, S = pltpu.VMEM, pltpu.SMEM
    rows = 2 * SIDE
    flat = ((rows, LANES), jnp.float32, V)
    work = [pltpu.VMEM((SIDE, SIDE), jnp.float32)]
    product_flops = 3 * 2 * SIDE**3

    devices = lax.axis_size(AXES)
    order = [
        sum((row >> k & 1) << bit for k, bit in enumerate(CHIP_BITS)) ^ FLIP for row in range(SIDE)
    ]
    chips = [[2 * chip + core for chip in order] for core in range(2)]

    def across(value):
        value = value.reshape(SIDE, SIDE)
        value = lax.all_to_all(value, AXES, 0, 0, tiled=True, axis_index_groups=chips)
        return value.reshape(rows, LANES)

    def beside(value):
        return lax.ppermute(value, AXES, [(d, d ^ 1) for d in range(devices)])

    fetched = [
        pltpu.VMEM((rows, LANES), jnp.float32),
        pltpu.SMEM(angles.shape, jnp.float32),
        pltpu.SMEM(pairings.shape, jnp.int32),
        pltpu.SemaphoreType.DMA((3,)),
    ]
    state, plan = call(
        first_kernel,
        [pltpu.HBM] * 3,
        [flat, ((26,), jnp.int32, S)],
        work + fetched,
        3 * product_flops,
        60,
    )(angles, pairings, initial_state.reshape(rows, LANES))
    state = across(state)
    prepared = call(
        prepare_kernel,
        [S, S, S],
        [
            ((4, SIDE, SIDE), jnp.bfloat16, V),
            ((4, SIDE, SIDE), jnp.bfloat16, V),
            ((4, SIDE, SIDE), jnp.float32, V),
            ((3, SIDE, SIDE), jnp.bfloat16, V),
            ((3, SIDE, SIDE), jnp.bfloat16, V),
            ((2, SIDE, SIDE), jnp.float32, V),
            ((16, LANES), jnp.float32, V),
        ],
        [pltpu.SMEM((25,), jnp.int32)],
        40 * product_flops,
        16,
    )(angles, pairings, plan)
    stuck = plan[0] != 0
    state, stuck, prepared = lax.optimization_barrier((state, stuck, prepared))
    square = ((SIDE, SIDE), jnp.float32, V)
    (begun,) = call(begin_kernel, [V] * 3, [square], [], product_flops, 16)(state, *prepared[:2])
    table = prepared[6]
    (state,) = call(second_kernel, [V] * 6, [flat], [], 7 * product_flops, 16)(
        begun, beside(state), *prepared[:3], table
    )
    state, stuck = lax.optimization_barrier((across(state), stuck))

    def third(value, front, back):
        kernel = functools.partial(third_kernel, front, back)
        return call(kernel, [S] + [V] * 4, [flat], work, 3 * product_flops, 16)(
            plan, *prepared[3:6], value
        )[0]

    def finish(value):
        return third(value, True, True).reshape(-1)

    def finish_slowly(value):
        value = third(value, True, False)
        device = lax.axis_index(AXES)
        for bit in range(9):
            route = [(d, d ^ 1 << bit) for d in range(devices)]
            other = lax.ppermute(value, AXES, route)
            c, s = table[3, LOCAL + bit], table[11, LOCAL + bit]
            upper = lax.shift_right_logical(device, bit) & 1 == 1
            value = c * value + jnp.where(upper, s, -s) * other
        return third(value, False, True).reshape(-1)

    return lax.cond(stuck, finish_slowly, finish, state)


def solution(mesh):
    return jax.shard_map(
        shards,
        mesh=mesh,
        in_specs=(P(AXES), P(), P()),
        out_specs=P(AXES),
        check_vma=False,
    )
```
